512 devices in a mesh: recv: 32 (over z, y_lo), tm: 16 (over x, y_hi, core).
Axes of the slice: x: 4, y: 8 (y_hi: 2, y_lo: 4; y = y_hi * 4 + y_lo), z: 8, core: 2. Of those that a mesh axis runs over, the one named last changes fastest.
Arguments:
- spectra: bfloat16 [2, 512, 256, 512], P(None, 'tm', 'recv'), may hold values from -6 to 6
- owners: int32 [4], replicated, may hold values from 0 to 31
- source_slots: int32 [4, 8], replicated, may hold values from 0 to 7, as said below
Outputs:
- correlations: float32 [32, 256, 512], P('tm', 'recv')
The draws below stay inside these ranges and needn't reach their ends.
Inputs may be any that keep to these rules, and one draw needn't show every extreme that they name: Block k of sources lies among the channels of recv index owners[k]. `source_slots`: the 8 slots of one block are distinct.
All inputs are finite; a program needn't handle non-finite values.
Results may differ from the reference program's by a relative error of at most 0.0019.
Values may be sent and summed in bfloat16 or wider, within the bound.
No kernel may reach another device: no remote copies, remote signals or barrier semaphores. Data moves between devices by JAX's collectives and lax.ppermute only.
A program may use at most 64 MiB of HBM per device.

```python
import jax
import jax.numpy as jnp
from jax import lax

F = 512
HALF = 64
RECV_DEV = 8
STEPS = 4
SB = 8
SOURCES = 32
WINDOWS = 512
RECEIVERS = 256
N_RECV = 32


def draw_source_slots(key, part):
    key = jax.random.fold_in(key, 7)
    step_keys = jax.random.split(key, STEPS)
    chosen = jax.vmap(lambda one_key: jax.random.permutation(one_key, RECV_DEV)[:SB])(step_keys)
    return chosen.astype(jnp.int32)


def touch_ends(drawn, stream_key, smallest, largest):
    dims = drawn.shape
    spot = [jax.random.randint(jax.random.fold_in(stream_key, axis), (), 0, dims[axis]) for axis in range(len(dims))]
    drawn = drawn.at[tuple(spot)].set(smallest)
    longest = dims.index(max(dims))
    spot[longest] = (spot[longest] + 1) % dims[longest]
    return drawn.at[tuple(spot)].set(largest)


def block_scale(key, dims, pieces, least, top_value):
    def one(dim, shards_of):
        steps = jax.random.uniform(jax.random.fold_in(jax.random.fold_in(key, 6), dim), (shards_of,), jnp.float32, least / len(pieces), top_value / len(pieces))
        return jnp.repeat(jnp.exp(steps), dims[dim] // shards_of).reshape((-1,) + (1,) * (len(dims) - dim - 1))

    loudness = one(*pieces[0])
    for cut in pieces[1:]:
        loudness = loudness * one(*cut)
    return loudness


def scatter_about(rng, extent, scale, reach, cuts=(), dtype=jnp.bfloat16):
    level = block_scale(rng, extent, cuts, -0.22, 0.18) if cuts else 1.0
    array = jax.random.normal(rng, extent, jnp.float32) * scale * level
    return jnp.minimum(jnp.maximum(array, -reach), reach).astype(dtype)


def setup_inputs(seed: int = 0) -> dict:
    key_of = jax.random.split(jax.random.key(seed), 4)
    return {
        "spectra": scatter_about(key_of[0], (2, WINDOWS, RECEIVERS, F), 1.0, 6.0, ((1, 16), (2, 32))),
        "owners": touch_ends(jax.random.randint(key_of[1], (STEPS,), 0, N_RECV), jax.random.fold_in(key_of[1], 1), 0, N_RECV - 1).astype(jnp.int32),
        "source_slots": draw_source_slots(jax.random.fold_in(key_of[3], 71), 0),
    }


epsilon = 1e-05

def band_matrix():
    positions = jnp.arange(F)
    near = (jnp.abs(positions[:, None] - positions[None, :]) <= HALF).astype(jnp.float32)
    return near / lax.optimization_barrier(jnp.sum(near, axis=0, keepdims=True))

def whiten(block, band_table):
    parts = block.astype(jnp.float32)
    energy = parts[0] * parts[0] + parts[1] * parts[1]
    smooth = jnp.matmul(energy, band_table, precision=lax.Precision.HIGHEST)
    return (parts * lax.rsqrt(smooth + epsilon)[None]).astype(jnp.bfloat16)

def reference(spectra, owners, source_slots):
    band_table = band_matrix()
    channel = (owners[:, None] * RECV_DEV + source_slots).reshape(-1).astype(jnp.int32)
    source = whiten(jnp.take(spectra, channel, axis=2), band_table).astype(jnp.float32)
    high = lax.Precision.HIGHEST

    def one_block(number):
        block = lax.dynamic_slice_in_dim(spectra, number * RECV_DEV, RECV_DEV, 2)
        whitened = whiten(block, band_table).astype(jnp.float32)
        cross_real = jnp.einsum('wsf,wrf->srf', source[0], whitened[0], precision=high) + jnp.einsum('wsf,wrf->srf', source[1], whitened[1], precision=high)
        cross_imag = jnp.einsum('wsf,wrf->srf', source[0], whitened[1], precision=high) - jnp.einsum('wsf,wrf->srf', source[1], whitened[0], precision=high)
        return jnp.real(jnp.fft.ifft(cross_real + 1j * cross_imag, axis=-1)).astype(jnp.float32)
    lag_blocks = lax.map(one_block, jnp.arange(N_RECV))
    return jnp.transpose(lag_blocks, (1, 0, 2, 3)).reshape(SOURCES, RECEIVERS, F)
```

```python
import functools

import jax
import jax.numpy as jnp
import ml_dtypes
import numpy as np
from jax import lax
from jax.experimental import pallas as pl
from jax.experimental.pallas import tpu as pltpu
from jax.sharding import PartitionSpec as P

F = 512
HALF = 64
N_RECV = 32
N_TM = 16
RECV_DEV = 8
WIN = 32
PAIRS = 8
EPSILON = 1e-05
INTERPRET = False

f32 = jnp.float32
bf16 = jnp.bfloat16


def bin_order():
    order = []
    for j in range(N_RECV):
        mine = [PAIRS * j + p for p in range(PAIRS)]
        order += mine + [F // 2 if f == 0 else F - f for f in mine]
    return np.array(order)


def tables():
    index = np.arange(F)
    near = np.abs(index[:, None] - index[None, :]) <= HALF
    counts = near.sum(0).astype(np.float32)[None, :]
    order = (bin_order()[:, None] == index[None, :]).astype(ml_dtypes.bfloat16)
    c, w, r = np.meshgrid(np.arange(2), np.arange(WIN), np.arange(RECV_DEV), indexing="ij")
    goes_to = (r * 2 * WIN + c * WIN + w).reshape(-1)
    lanes = (goes_to[:, None] == np.arange(2 * WIN * RECV_DEV)[None, :]).astype(ml_dtypes.bfloat16)
    lag = np.arange(F)
    wave = np.zeros((N_RECV, PAIRS, 2, F))
    for j in range(N_RECV):
        for p in range(PAIRS):
            f = PAIRS * j + p
            angle = 2 * np.pi * ((f * lag) % F) / F
            if f == 0:
                wave[j, p, 0] = 1.0
                wave[j, p, 1] = 1.0 - 2.0 * (lag % 2)
            else:
                wave[j, p, 0] = np.cos(angle)
                wave[j, p, 1] = -np.sin(angle)
    wave = (wave / F).reshape(F, F)
    high = wave.astype(ml_dtypes.bfloat16)
    low = (wave - high.astype(np.float64)).astype(ml_dtypes.bfloat16)
    blocks = [m.astype(ml_dtypes.bfloat16).reshape(F // 8, 8, F) for m in (near, order, lanes, high, low)]
    return [jnp.asarray(m) for m in (*blocks, counts)]


def table(ref):
    return ref[...].reshape(F, F)


def dot(a, b):
    return lax.dot_general(a, b, (((1,), (0,)), ((), ())), preferred_element_type=f32)


def dot_nt(a, b):
    return lax.dot_general(a, b, (((1,), (1,)), ((), ())), preferred_element_type=f32)


def whiten_kernel(x_ref, near_ref, order_ref, lanes_ref, counts_ref, y_ref):
    rows = WIN * RECV_DEV
    re = x_ref[0].astype(f32).reshape(rows, F)
    im = x_ref[1].astype(f32).reshape(rows, F)
    energy = re * re + im * im
    near = table(near_ref)
    first = energy.astype(bf16)
    rest = energy - first.astype(f32)
    second = rest.astype(bf16)
    third = (rest - second.astype(f32)).astype(bf16)
    total = dot(first, near) + (dot(second, near) + dot(third, near))
    scale = lax.rsqrt(total / counts_ref[...] + EPSILON)
    white = jnp.concatenate([(re * scale).astype(bf16), (im * scale).astype(bf16)], axis=0)
    turned = dot_nt(table(order_ref), white).astype(bf16)
    y_ref[...] = dot(turned, table(lanes_ref)).astype(bf16).reshape(y_ref.shape)


def cross_kernel(owners_ref, slots_ref, place_ref, y_ref, z_ref, wide):
    for g in range(4):
        wide[g] = y_ref[:, :, 128 * g : 128 * (g + 1)].astype(f32).reshape(wide.shape[1:])
    lane8 = lax.broadcasted_iota(jnp.int32, (8, 128), 1)
    odd_source = (lax.broadcasted_iota(jnp.int32, (8, 128), 0) // 2) % 2 == 1
    even_rows, odd_rows = [], []
    for t in range(N_TM):
        keys = []
        for s in (2 * t, 2 * t + 1):
            slot = slots_ref[s // 8, s % 8]
            keys.append((slot // 2) * N_RECV + owners_ref[s // 8] + 128 * (slot % 2))
        key = jnp.where(odd_source, keys[1], keys[0])
        even_rows.append(key == lane8)
        odd_rows.append(key - 128 == lane8)
    pick = jnp.concatenate(
        [
            jnp.concatenate([m.astype(f32) for m in even_rows], axis=0),
            jnp.concatenate([m.astype(f32) for m in odd_rows], axis=0),
        ],
        axis=1,
    ).astype(bf16)

    row = lax.broadcasted_iota(jnp.int32, (128, 128), 0)
    lane = lax.broadcasted_iota(jnp.int32, (128, 128), 1)
    second_part = (row // 4) % 2 == 1
    same_half = (row % 2) == (lane // 64)
    real_lane = (lane // 32) % 2 == 0
    low_lane = lane < 64
    is_first = place_ref[0] == 0
    halves = []
    for p in range(PAIRS):
        sides = []
        picked = []
        for sign in range(2):
            blocks = [
                wide.at[g][pl.ds(p + PAIRS * sign, N_RECV, stride=2 * PAIRS), :]
                for g in range(4)
            ]
            side = jnp.concatenate(blocks, axis=0)
            stacked = jnp.concatenate(
                [jnp.where(low_lane, side, 0.0), jnp.where(low_lane, 0.0, side)], axis=0
            ).astype(bf16)
            sides.append(side.astype(bf16))
            found = dot(pick, stacked)
            source = found + pltpu.roll(found, 64, 1)
            turned = pltpu.roll(source, 32, 1)
            turned = jnp.where(real_lane, -turned, turned)
            if sign:
                turned = -turned
            if p == 0:
                if sign:
                    first_part = jnp.where(is_first, 0.0, source)
                    turned = jnp.where(is_first, source, turned)
                else:
                    first_part = source
                    turned = jnp.where(is_first, 0.0, turned)
            else:
                first_part = source
            left = jnp.where(second_part, turned, first_part)
            picked.append(jnp.where(same_half, left, 0.0).astype(bf16))
        out = dot_nt(jnp.concatenate(picked, axis=1), jnp.concatenate(sides, axis=1))
        halves.append(out.reshape(N_TM, 8, 128))
        if p % 2:
            z_ref[:, 8 * (p - 1) : 8 * (p + 1), :] = jnp.concatenate(halves, axis=1).astype(bf16)
            halves = []


def gather_kernel(z_ref, q_ref, total):
    total[...] = jnp.sum(z_ref[...].astype(f32), axis=0)
    parts = [total[pl.ds(k, 16, stride=4), :] for k in range(4)]
    tall = jnp.concatenate(parts + [jnp.zeros((64, 128), f32)], axis=0)
    turned = tall.T
    for r in range(RECV_DEV):
        g = r // 2
        q_ref[:, r, :] = turned[N_RECV * g : N_RECV * (g + 1), :]


def lags_kernel(q_ref, high_ref, low_ref, out_ref):
    lane = lax.broadcasted_iota(jnp.int32, (8, 128), 1) // 16
    odd_row = lax.broadcasted_iota(jnp.int32, (8, 128), 0) % 2 == 1
    rows = []
    for s in range(2):
        tiles = []
        for q in range(4):
            tile = jnp.zeros((8, 128), f32)
            for i in range(8):
                block = q_ref[8 * q + i]
                here = []
                for k in (2 * s, 2 * s + 1):
                    shift = (16 * (i - k)) % 128
                    here.append(pltpu.roll(block, shift, 1) if shift else block)
                tile = jnp.where(lane == i, jnp.where(odd_row, here[1], here[0]), tile)
            tiles.append(tile)
        rows.append(jnp.concatenate(tiles, axis=1))
    value = jnp.concatenate(rows, axis=0)
    first = value.astype(bf16)
    second = (value - first.astype(f32)).astype(bf16)
    both = dot(jnp.concatenate([first, second], axis=0), table(high_ref))
    out_ref[...] = (both[:16] + (both[16:] + dot(first, table(low_ref)))).reshape(out_ref.shape)


def call(kernel, shape, dtype, operands, scratch=(), scalars=0):
    vmem = pl.BlockSpec(memory_space=pltpu.VMEM)
    smem = pl.BlockSpec(memory_space=pltpu.SMEM)
    return pl.pallas_call(
        kernel,
        out_shape=jax.ShapeDtypeStruct(shape, dtype),
        in_specs=[smem] * scalars + [vmem] * (len(operands) - scalars),
        out_specs=vmem,
        scratch_shapes=list(scratch),
        compiler_params=pltpu.CompilerParams(vmem_limit_bytes=32 << 20),
        interpret=INTERPRET,
    )(*operands)


def whiten(spectra):
    near, order, lanes, _, _, counts = tables()
    return call(
        whiten_kernel,
        (N_RECV, 2 * PAIRS, 2 * WIN * RECV_DEV),
        bf16,
        [spectra, near, order, lanes, counts],
    )


def cross(owners, source_slots, place, channels):
    return call(
        cross_kernel,
        (N_TM, 8 * PAIRS, 128),
        bf16,
        [owners, source_slots, place, channels],
        [pltpu.VMEM((4, N_RECV * 2 * PAIRS, 128), f32)],
        scalars=3,
    )


def gather(partial):
    return call(gather_kernel, (N_RECV, 8, 128), f32, [partial], [pltpu.VMEM((64, 128), f32)])


def lags(dofs):
    _, _, _, high, low, _ = tables()
    return call(lags_kernel, (2, RECV_DEV, F), f32, [dofs, high, low])


def per_device(spectra, owners, source_slots):
    exchange = functools.partial(lax.all_to_all, split_axis=0, concat_axis=0, tiled=True)
    place = lax.axis_index("recv").astype(jnp.int32).reshape(1)
    channels = exchange(whiten(spectra), "recv")
    partial = exchange(cross(owners, source_slots, place, channels), "tm")
    return lags(exchange(gather(partial), "recv"))


def solution(mesh):
    in_specs = (P(None, "tm", "recv", None), P(), P())
    out_specs = P("tm", "recv", None)
    return jax.shard_map(
        per_device, mesh=mesh, in_specs=in_specs, out_specs=out_specs, check_vma=False
    )
```

```python
import functools

import jax
import jax.numpy as jnp
import ml_dtypes
import numpy as np
from jax import lax
from jax.experimental import pallas as pl
from jax.experimental.pallas import tpu as pltpu
from jax.sharding import Mesh
from jax.sharding import PartitionSpec as P

F = 512
HALF = 64
N_RECV = 32
N_TM = 16
RECV_DEV = 8
WIN = 32
PAIRS = 8
EPSILON = 1e-05
INTERPRET = False

RECV = ("z", "y_lo")
TM = ("x", "y_hi", "core")
SIZES = {"z": 8, "y_lo": 4, "x": 4, "y_hi": 2, "core": 2}

f32 = jnp.float32
bf16 = jnp.bfloat16


def transform_table():
    lag = np.arange(F)
    wave = np.zeros((2, PAIRS, N_RECV, F))
    for j in range(N_RECV):
        for p in range(PAIRS):
            f = PAIRS * j + p
            angle = 2 * np.pi * ((f * lag) % F) / F
            if f == 0:
                wave[0, p, j] = 1.0
                wave[1, p, j] = 1.0 - 2.0 * (lag % 2)
            else:
                wave[0, p, j] = np.cos(angle)
                wave[1, p, j] = -np.sin(angle)
    wave = (wave / F).reshape(F // 8, 8, F)
    high = wave.astype(ml_dtypes.bfloat16)
    low = (wave - high.astype(np.float64)).astype(ml_dtypes.bfloat16)
    return jnp.asarray(high), jnp.asarray(low)


def dot(a, b):
    return lax.dot_general(a, b, (((1,), (0,)), ((), ())), preferred_element_type=f32)


def dot_nt(a, b):
    return lax.dot_general(a, b, (((1,), (1,)), ((), ())), preferred_element_type=f32)


def iota(shape, dim):
    return lax.broadcasted_iota(jnp.int32, shape, dim)


def ones_where(mask):
    return jnp.where(mask, 1.0, 0.0).astype(bf16)


def tm_place(t):
    return (t // 4) * 4 + (t % 2) * 2 + (t // 2) % 2


def band():
    gap = iota((128, 128), 0) - iota((128, 128), 1)
    inside = ones_where(jnp.abs(gap) <= HALF)
    above = ones_where(gap >= HALF)
    below = ones_where(gap <= -HALF)
    nothing = jnp.zeros((128, 128), bf16)
    pieces = {0: inside, 1: above, -1: below}
    rows = [
        jnp.concatenate([pieces.get(b - a, nothing) for b in range(4)], axis=1) for a in range(4)
    ]
    return jnp.concatenate(rows, axis=0)


def source_picker(owners_ref, slots_ref, pick_ref):
    sub = iota((8, 128), 0)
    lane = iota((8, 128), 1)
    for odd in range(2):
        for half in range(2):
            key = jnp.zeros((8, 128), jnp.int32)
            for t in range(N_TM):
                place = tm_place(t)
                if place // 8 != half:
                    continue
                s = 2 * t + odd
                channel = owners_ref[s // 8] * RECV_DEV + slots_ref[s // 8, s % 8]
                key = jnp.where(sub == place % 8, channel, key)
            found = jnp.concatenate(
                [jnp.where(key == lane, 1.0, 0.0), jnp.where(key == lane + 128, 1.0, 0.0)], axis=1
            )
            for dof in range(2):
                row = (2 * odd + dof) * N_TM + 8 * half
                pick_ref[row : row + 8, :] = found


def whiten_kernel(
    x_hbm, owners_hbm, slots_hbm, y_ref, pick_ref, x_ref, owners_ref, slots_ref, tall, pick, sems
):
    is_first = lax.axis_index(RECV) == 0
    copies = [
        pltpu.make_async_copy(owners_hbm, owners_ref, sems.at[4]),
        pltpu.make_async_copy(slots_hbm, slots_ref, sems.at[5]),
    ]
    for c in range(2):
        for part in range(2):
            here = pl.ds(part * WIN // 2, WIN // 2)
            copies.append(
                pltpu.make_async_copy(x_hbm.at[c, here], x_ref.at[c, here], sems.at[2 * c + part])
            )
    for copy in copies:
        copy.start()

    near = band()
    bins = iota((8, F), 1)
    counts = (jnp.minimum(bins + HALF, F - 1) - jnp.maximum(bins - HALF, 0) + 1).astype(f32)
    row = iota((256, 256), 0)
    column = iota((256, 256), 1)
    forward = ones_where(row == column)
    backward = ones_where((row + column) % 256 == 0)
    source_row = iota((F, 128), 0)
    goes_to = (source_row % 8) * 64 + source_row // 8
    lane = iota((F, 128), 1)
    lanes = jnp.concatenate([ones_where(goes_to == lane + 128 * b) for b in range(4)], axis=1)

    for copy in copies:
        copy.wait()
    source_picker(owners_ref, slots_ref, pick)
    pick[64:80, :] = jnp.full((16, 256), jnp.where(is_first, 1.0, 0.0), f32)
    pick_ref[...] = pick[...].astype(bf16)

    rows = WIN * RECV_DEV
    re = x_ref[0].astype(f32).reshape(rows, F)
    im = x_ref[1].astype(f32).reshape(rows, F)
    energy = re * re + im * im
    first = energy.astype(bf16)
    rest = energy - first.astype(f32)
    second = rest.astype(bf16)
    third = (rest - second.astype(f32)).astype(bf16)
    total = dot(first, near) + (dot(second, near) + dot(third, near))
    scale = lax.rsqrt(total * (1.0 / counts)[:1] + EPSILON)
    white = jnp.concatenate([(re * scale).astype(bf16), (im * scale).astype(bf16)], axis=0)
    ahead = dot(dot_nt(forward, white[:, :256]).astype(bf16), lanes)
    behind = dot(dot_nt(backward, white[:, 256:]).astype(bf16), lanes)
    low = iota((256, 128), 1) < 64
    for g in range(4):
        one = ahead[:, 128 * g : 128 * (g + 1)]
        two = behind[:, 128 * g : 128 * (g + 1)]
        tall[pl.ds(2 * g, 256, stride=8), :] = jnp.where(low, one, pltpu.roll(two, 64, 1))
        tall[pl.ds(2 * g + 1, 256, stride=8), :] = jnp.where(low, pltpu.roll(one, 64, 1), two)
    y_ref[...] = tall[...].astype(bf16).reshape(y_ref.shape)


def cross_kernel(pick_ref, y_ref, z_ref, wide):
    pick = pick_ref[:64, :]
    is_first = pick_ref[64:80, :128].astype(f32)[:1] > 0.5
    row = iota((64, 128), 0)
    lane = iota((64, 128), 1)
    imaginary = (row // N_TM) % 2 == 1
    real_lane = (lane // 32) % 2 == 0
    ahead = lane < 64
    sign = jnp.where(real_lane == ahead, -1.0, 1.0)
    for p in range(PAIRS):
        if p % 2 == 0:
            two = y_ref[:, 8 * p : 8 * p + 16, :].astype(f32)
        side = two[:, 8 * (p % 2) : 8 * (p % 2) + 8, :].reshape(256, 128).astype(bf16)
        source = dot(pick, side)
        turned = sign * jnp.where(real_lane, pltpu.roll(source, 96, 1), pltpu.roll(source, 32, 1))
        left = jnp.where(imaginary, turned, source)
        if p == 0:
            ends = jnp.where(imaginary == ahead, 0.0, source)
            left = jnp.where(is_first, ends, left)
        out = dot_nt(left.astype(bf16), side)
        for q in range(4):
            for h in range(2):
                wide.at[h][pl.ds(8 * q + p, N_TM, stride=32), :] = out[
                    N_TM * q : N_TM * (q + 1), 128 * h : 128 * (h + 1)
                ]
    for h in range(2):
        z_ref[:, :, 128 * h : 128 * (h + 1)] = wide[h].astype(bf16).reshape(8, 64, 128)


def gather_kernel(z_ref, q_ref, tall, flat):
    total = jnp.sum(z_ref[...].astype(f32), axis=0)
    for h in range(2):
        block = total[:, 128 * h : 128 * (h + 1)]
        tall[128 * h : 128 * (h + 1), :] = jnp.concatenate([block, jnp.zeros_like(block)], axis=0).T
    group = iota((N_RECV, 128), 1) // 32
    for h in range(2):
        channels = [tall[pl.ds(4 * h + r, N_RECV, stride=8), :] for r in range(4)]
        for y in range(2):
            packed = jnp.zeros((N_RECV, 128), f32)
            for r in range(4):
                moved = channels[r]
                if r != y:
                    moved = pltpu.roll(moved, (32 * (r - y)) % 128, 1)
                packed = jnp.where(group == r, moved, packed)
            flat.at[h][pl.ds(y, N_RECV, stride=2), :] = packed
    for h in range(2):
        q_ref[:, h, :] = flat[h]


def lags_kernel(q_ref, high_ref, low_ref, out_ref, flat, turned, mixed):
    for h in range(2):
        flat.at[h][...] = q_ref[:, h, :]
    sums = []
    for h in range(2):
        sums.append(
            flat.at[h][pl.ds(0, N_RECV, stride=2), :] + flat.at[h][pl.ds(1, N_RECV, stride=2), :]
        )
    turned[...] = jnp.concatenate(sums + [jnp.zeros((64, 128), f32)], axis=0).T
    group = iota((8, 128), 1) // 32
    rows = [[], []]
    for q in range(4):
        tiles = [jnp.zeros((8, 128), f32) for _ in range(2)]
        for i in range(4):
            block = turned[pl.ds(4 * q + i, 8, stride=16), :]
            for h in range(2):
                moved = pltpu.roll(block, (32 * (i - h)) % 128, 1) if i != h else block
                tiles[h] = jnp.where(group == i, moved, tiles[h])
        for h in range(2):
            rows[h].append(tiles[h])
    value = jnp.concatenate([jnp.concatenate(r, axis=1) for r in rows], axis=0)
    first = value.astype(bf16)
    second = (value - first.astype(f32)).astype(bf16)
    high = high_ref[...].reshape(F, F)
    low = low_ref[...].reshape(F, F)
    both = dot(jnp.concatenate([first, second], axis=0), high)
    lags = both[:16] + (both[16:] + dot(first, low))
    for b in range(4):
        mixed.at[b][...] = lags[:, 128 * b : 128 * (b + 1)]
    for s in range(2):
        for b in range(4):
            out_ref[s, :, 128 * b : 128 * (b + 1)] = mixed.at[b][pl.ds(s, 8, stride=2), :]


VMEM = pl.BlockSpec(memory_space=pltpu.VMEM)
SMEM = pl.BlockSpec(memory_space=pltpu.SMEM)
HBM = pl.BlockSpec(memory_space=pl.ANY)


def call(kernel, outs, operands, specs, scratch=(), grant=32):
    return pl.pallas_call(
        kernel,
        out_shape=outs,
        in_specs=specs,
        out_specs=jax.tree.map(lambda _: VMEM, outs),
        scratch_shapes=list(scratch),
        compiler_params=pltpu.CompilerParams(vmem_limit_bytes=grant << 20),
        interpret=INTERPRET,
    )(*operands)


def whiten(spectra, owners, source_slots):
    return call(
        whiten_kernel,
        (
            jax.ShapeDtypeStruct((N_RECV, PAIRS * RECV_DEV, 128), bf16),
            jax.ShapeDtypeStruct((80, 256), bf16),
        ),
        [spectra, owners, source_slots],
        [HBM] * 3,
        [
            pltpu.VMEM((2, WIN, RECV_DEV, F), bf16),
            pltpu.SMEM((4,), jnp.int32),
            pltpu.SMEM((4, 8), jnp.int32),
            pltpu.VMEM((N_RECV * PAIRS * RECV_DEV, 128), f32),
            pltpu.VMEM((80, 256), f32),
            pltpu.SemaphoreType.DMA((6,)),
        ],
        grant=53,
    )


def cross(pick, channels):
    return call(
        cross_kernel,
        jax.ShapeDtypeStruct((8, 64, 256), bf16),
        [pick, channels],
        [VMEM, VMEM],
        [pltpu.VMEM((2, 512, 128), f32)],
    )


def gather(partial):
    return call(
        gather_kernel,
        jax.ShapeDtypeStruct((2 * N_RECV, 2, 128), f32),
        [partial],
        [VMEM],
        [pltpu.VMEM((256, 128), f32), pltpu.VMEM((2, 64, 128), f32)],
    )


def lags(dofs):
    return call(
        lags_kernel,
        jax.ShapeDtypeStruct((2, RECV_DEV, F), f32),
        [dofs, *transform_table()],
        [VMEM] * 3,
        [pltpu.VMEM((2, 64, 128), f32), pltpu.VMEM((128, 128), f32), pltpu.VMEM((4, 16, 128), f32)],
    )


def per_device(spectra, owners, source_slots):
    exchange = functools.partial(lax.all_to_all, split_axis=0, concat_axis=0, tiled=True)
    mine, pick = whiten(spectra, owners, source_slots)
    channels = exchange(mine, RECV)
    partial = exchange(cross(pick, channels), ("x", "core"))
    return lags(exchange(gather(partial), (*RECV, "y_hi")))


def solution(mesh):
    names = (*RECV, *TM)
    fine = Mesh(mesh.devices.reshape([SIZES[n] for n in names]), names)
    in_specs = (P(None, TM, RECV, None), P(), P())
    out_specs = P(TM, RECV, None)
    return jax.shard_map(
        per_device, mesh=fine, in_specs=in_specs, out_specs=out_specs, check_vma=False
    )
```

```python
import functools

import jax
import jax.numpy as jnp
import ml_dtypes
import numpy as np
from jax import lax
from jax.experimental import pallas as pl
from jax.experimental.pallas import tpu as pltpu
from jax.sharding import Mesh
from jax.sharding import PartitionSpec as P

F = 512
HALF = 64
N_RECV = 32
N_TM = 16
RECV_DEV = 8
WIN = 32
PAIRS = 8
EPSILON = 1e-05
CHUNKS = 2
INTERPRET = False

RECV = ("z", "y_lo")
TM = ("x", "y_hi", "core")
SIZES = {"z": 8, "y_lo": 4, "x": 4, "y_hi": 2, "core": 2}

f32 = jnp.float32
bf16 = jnp.bfloat16


def transform_table():
    lag = np.arange(F)
    wave = np.zeros((2, PAIRS, N_RECV, F))
    for j in range(N_RECV):
        for p in range(PAIRS):
            f = PAIRS * j + p
            angle = 2 * np.pi * ((f * lag) % F) / F
            if f == 0:
                wave[0, p, j] = 1.0
                wave[1, p, j] = 1.0 - 2.0 * (lag % 2)
            else:
                wave[0, p, j] = np.cos(angle)
                wave[1, p, j] = -np.sin(angle)
    wave = (wave / F).reshape(F // 8, 8, F)
    high = wave.astype(ml_dtypes.bfloat16)
    low = (wave - high.astype(np.float64)).astype(ml_dtypes.bfloat16)
    return jnp.asarray(high), jnp.asarray(low)


def dot(a, b):
    return lax.dot_general(a, b, (((1,), (0,)), ((), ())), preferred_element_type=f32)


def dot_nt(a, b):
    return lax.dot_general(a, b, (((1,), (1,)), ((), ())), preferred_element_type=f32)


def iota(shape, dim):
    return lax.broadcasted_iota(jnp.int32, shape, dim)


def ones_where(mask):
    return jnp.where(mask, 1.0, 0.0).astype(bf16)


def tm_place(t):
    return (t // 4) * 4 + (t % 2) * 2 + (t // 2) % 2


def band():
    gap = iota((128, 128), 0) - iota((128, 128), 1)
    inside = ones_where(jnp.abs(gap) <= HALF)
    above = ones_where(gap >= HALF)
    below = ones_where(gap <= -HALF)
    nothing = jnp.zeros((128, 128), bf16)
    pieces = {0: inside, 1: above, -1: below}
    rows = [
        jnp.concatenate([pieces.get(b - a, nothing) for b in range(4)], axis=1) for a in range(4)
    ]
    return jnp.concatenate(rows, axis=0)


def source_picker(owners_ref, slots_ref, pick_ref):
    sub = iota((8, 128), 0)
    lane = iota((8, 128), 1)
    for odd in range(2):
        for half in range(2):
            key = jnp.zeros((8, 128), jnp.int32)
            for t in range(N_TM):
                place = tm_place(t)
                if place // 8 != half:
                    continue
                s = 2 * t + odd
                channel = owners_ref[s // 8] * RECV_DEV + slots_ref[s // 8, s % 8]
                key = jnp.where(sub == place % 8, channel, key)
            found = jnp.concatenate(
                [jnp.where(key == lane, 1.0, 0.0), jnp.where(key == lane + 128, 1.0, 0.0)], axis=1
            )
            for dof in range(2):
                row = (2 * odd + dof) * N_TM + 8 * half
                pick_ref[row : row + 8, :] = found


def whiten_kernel(
    x_hbm, owners_hbm, slots_hbm, y_ref, pick_ref, x_ref, owners_ref, slots_ref, white, tall, pick, sems
):
    is_first = lax.axis_index(RECV) == 0
    part = WIN // CHUNKS
    copies = [
        pltpu.make_async_copy(
            x_hbm.at[:, pl.ds(k * part, part)], x_ref.at[:, pl.ds(k * part, part)], sems.at[k]
        )
        for k in range(CHUNKS)
    ]
    small = [
        pltpu.make_async_copy(owners_hbm, owners_ref, sems.at[CHUNKS]),
        pltpu.make_async_copy(slots_hbm, slots_ref, sems.at[CHUNKS + 1]),
    ]
    for copy in copies + small:
        copy.start()

    near = band()
    bins = iota((8, F), 1)
    counts = (jnp.minimum(bins + HALF, F - 1) - jnp.maximum(bins - HALF, 0) + 1).astype(f32)
    share = (1.0 / counts)[:1]
    row = iota((256, 256), 0)
    column = iota((256, 256), 1)
    forward = ones_where(row == column)
    backward = ones_where((row + column) % 256 == 0)
    low = iota((256, 128), 1) < 64

    rows = part * RECV_DEV
    for k in range(CHUNKS):
        copies[k].wait()
        re, im = [
            x_ref[c, part * k : part * (k + 1)].astype(f32).reshape(rows, F) for c in range(2)
        ]
        energy = re * re + im * im
        first = energy.astype(bf16)
        second = (energy - first.astype(f32)).astype(bf16)
        total = dot(first, near) + dot(second, near)
        scale = lax.rsqrt(total * share + EPSILON)
        for c, value in enumerate((re, im)):
            start = (c * WIN + k * part) * RECV_DEV
            for b in range(4):
                white.at[b][start : start + rows, :] = (value * scale)[:, 128 * b : 128 * (b + 1)]

    for copy in small:
        copy.wait()
    source_picker(owners_ref, slots_ref, pick)
    pick[64:80, :] = jnp.full((16, 256), jnp.where(is_first, 1.0, 0.0), f32)
    pick_ref[...] = pick[...].astype(bf16)

    def by_channel(b):
        strips = [white.at[b][pl.ds(r, 2 * WIN, stride=RECV_DEV), :] for r in range(RECV_DEV)]
        return jnp.concatenate(strips, axis=0).astype(bf16)

    blocks = [by_channel(b) for b in range(4)]
    ahead = dot_nt(forward, jnp.concatenate(blocks[:2], axis=1))
    behind = dot_nt(backward, jnp.concatenate(blocks[2:], axis=1))
    for g in range(4):
        one = ahead[:, 128 * g : 128 * (g + 1)]
        two = behind[:, 128 * g : 128 * (g + 1)]
        tall[pl.ds(2 * g, 256, stride=8), :] = jnp.where(low, one, pltpu.roll(two, 64, 1))
        tall[pl.ds(2 * g + 1, 256, stride=8), :] = jnp.where(low, pltpu.roll(one, 64, 1), two)
    y_ref[...] = tall[...].astype(bf16).reshape(y_ref.shape)


def cross_kernel(pick_ref, y_ref, z_ref, wide):
    pick = pick_ref[:64, :]
    is_first = pick_ref[64:80, :128].astype(f32)[:1] > 0.5
    row = iota((64, 128), 0)
    lane = iota((64, 128), 1)
    imaginary = (row // N_TM) % 2 == 1
    real_lane = (lane // 32) % 2 == 0
    ahead = lane < 64
    sign = jnp.where(real_lane == ahead, -1.0, 1.0)
    for p in range(PAIRS):
        if p % 2 == 0:
            two = y_ref[:, 8 * p : 8 * p + 16, :].astype(f32)
        side = two[:, 8 * (p % 2) : 8 * (p % 2) + 8, :].reshape(256, 128).astype(bf16)
        source = dot(pick, side)
        turned = sign * jnp.where(real_lane, pltpu.roll(source, 96, 1), pltpu.roll(source, 32, 1))
        left = jnp.where(imaginary, turned, source)
        if p == 0:
            ends = jnp.where(imaginary == ahead, 0.0, source)
            left = jnp.where(is_first, ends, left)
        out = dot_nt(left.astype(bf16), side)
        for q in range(4):
            for h in range(2):
                wide.at[h][pl.ds(8 * q + p, N_TM, stride=32), :] = out[
                    N_TM * q : N_TM * (q + 1), 128 * h : 128 * (h + 1)
                ]
    for h in range(2):
        z_ref[:, :, 128 * h : 128 * (h + 1)] = wide[h].astype(bf16).reshape(8, 64, 128)


def gather_kernel(z_ref, q_ref, tall, flat):
    total = jnp.sum(z_ref[...].astype(f32), axis=0)
    for h in range(2):
        block = total[:, 128 * h : 128 * (h + 1)]
        tall[128 * h : 128 * (h + 1), :] = jnp.concatenate([block, jnp.zeros_like(block)], axis=0).T
    group = iota((N_RECV, 128), 1) // 32
    for h in range(2):
        channels = [tall[pl.ds(4 * h + r, N_RECV, stride=8), :] for r in range(4)]
        for y in range(2):
            packed = jnp.zeros((N_RECV, 128), f32)
            for r in range(4):
                moved = channels[r]
                if r != y:
                    moved = pltpu.roll(moved, (32 * (r - y)) % 128, 1)
                packed = jnp.where(group == r, moved, packed)
            flat.at[h][pl.ds(y, N_RECV, stride=2), :] = packed
    for h in range(2):
        q_ref[:, h, :] = flat[h]


def lags_kernel(q_ref, high_ref, low_ref, out_ref, flat, turned, mixed):
    for h in range(2):
        flat.at[h][...] = q_ref[:, h, :]
    sums = []
    for h in range(2):
        sums.append(
            flat.at[h][pl.ds(0, N_RECV, stride=2), :] + flat.at[h][pl.ds(1, N_RECV, stride=2), :]
        )
    turned[...] = jnp.concatenate(sums + [jnp.zeros((64, 128), f32)], axis=0).T
    group = iota((8, 128), 1) // 32
    rows = [[], []]
    for q in range(4):
        tiles = [jnp.zeros((8, 128), f32) for _ in range(2)]
        for i in range(4):
            block = turned[pl.ds(4 * q + i, 8, stride=16), :]
            for h in range(2):
                moved = pltpu.roll(block, (32 * (i - h)) % 128, 1) if i != h else block
                tiles[h] = jnp.where(group == i, moved, tiles[h])
        for h in range(2):
            rows[h].append(tiles[h])
    value = jnp.concatenate([jnp.concatenate(r, axis=1) for r in rows], axis=0)
    first = value.astype(bf16)
    second = (value - first.astype(f32)).astype(bf16)
    high = high_ref[...].reshape(F, F)
    low = low_ref[...].reshape(F, F)
    both = dot(jnp.concatenate([first, second], axis=0), high)
    lags = both[:16] + (both[16:] + dot(first, low))
    for b in range(4):
        mixed.at[b][...] = lags[:, 128 * b : 128 * (b + 1)]
    for s in range(2):
        for b in range(4):
            out_ref[s, :, 128 * b : 128 * (b + 1)] = mixed.at[b][pl.ds(s, 8, stride=2), :]


VMEM = pl.BlockSpec(memory_space=pltpu.VMEM)
HBM = pl.BlockSpec(memory_space=pltpu.HBM)


def call(kernel, outs, operands, specs, scratch=()):
    return pl.pallas_call(
        kernel,
        out_shape=outs,
        in_specs=specs,
        out_specs=jax.tree.map(lambda _: VMEM, outs),
        scratch_shapes=list(scratch),
        compiler_params=pltpu.CompilerParams(vmem_limit_bytes=32 << 20),
        interpret=INTERPRET,
    )(*operands)


def whiten(spectra, owners, source_slots):
    return call(
        whiten_kernel,
        (
            jax.ShapeDtypeStruct((N_RECV, PAIRS * RECV_DEV, 128), bf16),
            jax.ShapeDtypeStruct((80, 256), bf16),
        ),
        [pltpu.with_memory_space_constraint(a, pltpu.HBM) for a in (spectra, owners, source_slots)],
        [HBM] * 3,
        [
            pltpu.VMEM((2, WIN, RECV_DEV, F), bf16),
            pltpu.SMEM((4,), jnp.int32),
            pltpu.SMEM((4, 8), jnp.int32),
            pltpu.VMEM((4, 2 * WIN * RECV_DEV, 128), f32),
            pltpu.VMEM((N_RECV * PAIRS * RECV_DEV, 128), f32),
            pltpu.VMEM((80, 256), f32),
            pltpu.SemaphoreType.DMA((CHUNKS + 2,)),
        ],
    )


def cross(pick, channels):
    return call(
        cross_kernel,
        jax.ShapeDtypeStruct((8, 64, 256), bf16),
        [pick, channels],
        [VMEM, VMEM],
        [pltpu.VMEM((2, 512, 128), f32)],
    )


def gather(partial):
    return call(
        gather_kernel,
        jax.ShapeDtypeStruct((2 * N_RECV, 2, 128), f32),
        [partial],
        [VMEM],
        [pltpu.VMEM((256, 128), f32), pltpu.VMEM((2, 64, 128), f32)],
    )


def lags(dofs):
    return call(
        lags_kernel,
        jax.ShapeDtypeStruct((2, RECV_DEV, F), f32),
        [dofs, *transform_table()],
        [VMEM] * 3,
        [pltpu.VMEM((2, 64, 128), f32), pltpu.VMEM((128, 128), f32), pltpu.VMEM((4, 16, 128), f32)],
    )


def per_device(spectra, owners, source_slots):
    exchange = functools.partial(lax.all_to_all, split_axis=0, concat_axis=0, tiled=True)
    mine, pick = whiten(spectra, owners, source_slots)
    channels = exchange(mine, RECV)
    partial = exchange(cross(pick, channels), ("x", "core"))
    return lags(exchange(gather(partial), (*RECV, "y_hi")))


def solution(mesh):
    names = (*RECV, *TM)
    fine = Mesh(mesh.devices.reshape([SIZES[n] for n in names]), names)
    in_specs = (P(None, TM, RECV, None), P(), P())
    out_specs = P(TM, RECV, None)
    return jax.shard_map(
        per_device, mesh=fine, in_specs=in_specs, out_specs=out_specs, check_vma=False
    )
```

```python
import functools

import jax
import jax.numpy as jnp
import ml_dtypes
import numpy as np
from jax import lax
from jax.experimental import pallas as pl
from jax.experimental.pallas import tpu as pltpu
from jax.sharding import Mesh
from jax.sharding import PartitionSpec as P

F = 512
HALF = 64
N_RECV = 32
N_TM = 16
RECV_DEV = 8
WIN = 32
PAIRS = 8
EPSILON = 1e-05
CHUNKS = 2
PITCH = 40
INTERPRET = False

RECV = ("z", "y_lo")
TM = ("x", "y_hi", "core")
SIZES = {"z": 8, "y_lo": 4, "x": 4, "y_hi": 2, "core": 2}

f32 = jnp.float32
bf16 = jnp.bfloat16


def transform_table():
    lag = np.arange(F)
    wave = np.zeros((2, PAIRS, N_RECV, F))
    for j in range(N_RECV):
        for p in range(PAIRS):
            f = PAIRS * j + p
            angle = 2 * np.pi * ((f * lag) % F) / F
            if f == 0:
                wave[0, p, j] = 1.0
                wave[1, p, j] = 1.0 - 2.0 * (lag % 2)
            else:
                wave[0, p, j] = np.cos(angle)
                wave[1, p, j] = -np.sin(angle)
    wave = (wave / F).reshape(F // 8, 8, F)
    high = wave.astype(ml_dtypes.bfloat16)
    low = (wave - high.astype(np.float64)).astype(ml_dtypes.bfloat16)
    return jnp.asarray(high), jnp.asarray(low)


def dot(a, b):
    return lax.dot_general(a, b, (((1,), (0,)), ((), ())), preferred_element_type=f32)


def dot_nt(a, b):
    return lax.dot_general(a, b, (((1,), (1,)), ((), ())), preferred_element_type=f32)


def iota(shape, dim):
    return lax.broadcasted_iota(jnp.int32, shape, dim)


def ones_where(mask):
    return jnp.where(mask, 1.0, 0.0).astype(bf16)


def tm_place(t):
    return (t // 4) * 4 + (t % 2) * 2 + (t // 2) % 2


def band():
    gap = iota((128, 128), 0) - iota((128, 128), 1)
    inside = ones_where(jnp.abs(gap) <= HALF)
    above = ones_where(gap >= HALF)
    below = ones_where(gap <= -HALF)
    nothing = jnp.zeros((128, 128), bf16)
    pieces = {0: inside, 1: above, -1: below}
    rows = [
        jnp.concatenate([pieces.get(b - a, nothing) for b in range(4)], axis=1) for a in range(4)
    ]
    return jnp.concatenate(rows, axis=0)


def source_picker(owners_ref, slots_ref, pick_ref):
    sub = iota((8, 128), 0)
    lane = iota((8, 128), 1)
    for odd in range(2):
        for half in range(2):
            key = jnp.zeros((8, 128), jnp.int32)
            for t in range(N_TM):
                place = tm_place(t)
                if place // 8 != half:
                    continue
                s = 2 * t + odd
                channel = owners_ref[s // 8] * RECV_DEV + slots_ref[s // 8, s % 8]
                key = jnp.where(sub == place % 8, channel, key)
            found = jnp.concatenate(
                [jnp.where(key == lane, 1.0, 0.0), jnp.where(key == lane + 128, 1.0, 0.0)], axis=1
            )
            for dof in range(2):
                row = (2 * odd + dof) * N_TM + 8 * half
                pick_ref[row : row + 8, :] = found


def whiten_kernel(
    x_hbm, owners_hbm, slots_hbm, y_ref, pick_ref, x_ref, owners_ref, slots_ref, white, tall, pick, sems
):
    is_first = lax.axis_index(RECV) == 0
    part = WIN // CHUNKS
    copies = [
        pltpu.make_async_copy(
            x_hbm.at[:, pl.ds(k * part, part)], x_ref.at[:, pl.ds(k * part, part)], sems.at[k]
        )
        for k in range(CHUNKS)
    ]
    small = [
        pltpu.make_async_copy(owners_hbm, owners_ref, sems.at[CHUNKS]),
        pltpu.make_async_copy(slots_hbm, slots_ref, sems.at[CHUNKS + 1]),
    ]
    for copy in copies + small:
        copy.start()

    near = band()
    bins = iota((8, F), 1)
    counts = (jnp.minimum(bins + HALF, F - 1) - jnp.maximum(bins - HALF, 0) + 1).astype(f32)
    share = (1.0 / counts)[:1]
    row = iota((256, 256), 0)
    column = iota((256, 256), 1)
    forward = ones_where(row == column)
    backward = ones_where((row + column) % 256 == 0)
    low = iota((256, 128), 1) < 64

    rows = part * RECV_DEV
    for k in range(CHUNKS):
        copies[k].wait()
        re, im = [
            x_ref[c, part * k : part * (k + 1)].astype(f32).reshape(rows, F) for c in range(2)
        ]
        energy = re * re + im * im
        first = energy.astype(bf16)
        second = (energy - first.astype(f32)).astype(bf16)
        total = dot(first, near) + dot(second, near)
        scale = lax.rsqrt(total * share + EPSILON)
        for c, value in enumerate((re, im)):
            start = (c * WIN + k * part) * RECV_DEV
            for b in range(4):
                white.at[b][start : start + rows, :] = (value * scale)[:, 128 * b : 128 * (b + 1)]

    for copy in small:
        copy.wait()
    source_picker(owners_ref, slots_ref, pick)
    pick[64:80, :] = jnp.full((16, 256), jnp.where(is_first, 1.0, 0.0), f32)
    pick_ref[...] = pick[...].astype(bf16)

    def by_channel(b):
        strips = [white.at[b][pl.ds(r, 2 * WIN, stride=RECV_DEV), :] for r in range(RECV_DEV)]
        return jnp.concatenate(strips, axis=0).astype(bf16)

    blocks = [by_channel(b) for b in range(4)]
    ahead = dot_nt(forward, jnp.concatenate(blocks[:2], axis=1))
    behind = dot_nt(backward, jnp.concatenate(blocks[2:], axis=1))
    for g in range(4):
        one = ahead[:, 128 * g : 128 * (g + 1)]
        two = behind[:, 128 * g : 128 * (g + 1)]
        tall[pl.ds(2 * g, 256, stride=8), :] = jnp.where(low, one, pltpu.roll(two, 64, 1))
        tall[pl.ds(2 * g + 1, 256, stride=8), :] = jnp.where(low, pltpu.roll(one, 64, 1), two)
    y_ref[...] = tall[...].astype(bf16).reshape(y_ref.shape)


def cross_kernel(pick_ref, y_ref, z_ref, wide):
    pick = pick_ref[:64, :]
    is_first = pick_ref[64:80, :128].astype(f32)[:1] > 0.5
    lane = iota((N_TM, 128), 1)
    real_lane = (lane // 32) % 2 == 0
    ahead = lane < 64
    sign = jnp.where(real_lane == ahead, -1.0, 1.0)
    nothing = jnp.zeros((64, 128), f32)
    for pair in range(PAIRS // 2):
        two = y_ref[:, 16 * pair : 16 * pair + 16, :].astype(f32)
        side = jnp.concatenate(
            [two[:, 8 * i : 8 * i + 8, :].reshape(256, 128) for i in range(2)], axis=1
        ).astype(bf16)
        found = dot(pick, side)
        lefts = []
        for i in range(2):
            strips = []
            for q in range(4):
                strip = found[N_TM * q : N_TM * (q + 1), 128 * i : 128 * (i + 1)]
                first_bin = jnp.where(ahead == (q % 2 == 0), strip, 0.0)
                if q % 2:
                    strip = sign * jnp.where(
                        real_lane, pltpu.roll(strip, 96, 1), pltpu.roll(strip, 32, 1)
                    )
                if pair == 0 and i == 0:
                    strip = jnp.where(is_first, first_bin, strip)
                strips.append(strip)
            lefts.append(jnp.concatenate(strips, axis=0))
        left = jnp.concatenate(
            [
                jnp.concatenate([lefts[0], nothing], axis=1),
                jnp.concatenate([nothing, lefts[1]], axis=1),
            ],
            axis=0,
        )
        out = dot_nt(left.astype(bf16), side)
        for i in range(2):
            for q in range(4):
                row = 64 * i + N_TM * q
                for h in range(2):
                    wide.at[h][pl.ds(8 * q + 2 * pair + i, N_TM, stride=PITCH), :] = out[
                        row : row + N_TM, 128 * h : 128 * (h + 1)
                    ]
    for h in range(2):
        block = wide[h].reshape(N_TM, PITCH, 128)[:, :32, :]
        z_ref[:, :, 128 * h : 128 * (h + 1)] = block.astype(bf16).reshape(8, 64, 128)


def gather_kernel(z_ref, q_ref, tall):
    total = jnp.sum(z_ref[...].astype(f32), axis=0)
    for h in range(2):
        block = total[:, 128 * h : 128 * (h + 1)]
        tall[128 * h : 128 * (h + 1), :] = jnp.concatenate([block, jnp.zeros_like(block)], axis=0).T
    group = iota((N_RECV, 128), 1) // 32
    for h in range(2):
        channels = [tall[pl.ds(4 * h + r, N_RECV, stride=8), :] for r in range(4)]
        for y in range(2):
            packed = jnp.zeros((N_RECV, 128), f32)
            for r in range(4):
                moved = channels[r]
                if r != y:
                    moved = pltpu.roll(moved, (32 * (r - y)) % 128, 1)
                packed = jnp.where(group == r, moved, packed)
            q_ref[N_RECV * y : N_RECV * (y + 1), h, :] = packed


def lags_kernel(q_ref, high_ref, low_ref, out_ref, turned, mixed):
    sums = [q_ref[:N_RECV, h, :] + q_ref[N_RECV:, h, :] for h in range(2)]
    turned[...] = jnp.concatenate(sums + [jnp.zeros((64, 128), f32)], axis=0).T
    group = iota((8, 128), 1) // 32
    rows = [[], []]
    for q in range(4):
        tiles = [jnp.zeros((8, 128), f32) for _ in range(2)]
        for i in range(4):
            block = turned[pl.ds(4 * q + i, 8, stride=16), :]
            for h in range(2):
                moved = pltpu.roll(block, (32 * (i - h)) % 128, 1) if i != h else block
                tiles[h] = jnp.where(group == i, moved, tiles[h])
        for h in range(2):
            rows[h].append(tiles[h])
    value = jnp.concatenate([jnp.concatenate(r, axis=1) for r in rows], axis=0)
    first = value.astype(bf16)
    second = (value - first.astype(f32)).astype(bf16)
    high = high_ref[...].reshape(F, F)
    low = low_ref[...].reshape(F, F)
    both = dot(jnp.concatenate([first, second], axis=0), high)
    lags = both[:16] + (both[16:] + dot(first, low))
    for b in range(4):
        mixed.at[b][...] = lags[:, 128 * b : 128 * (b + 1)]
    for s in range(2):
        for b in range(4):
            out_ref[s, :, 128 * b : 128 * (b + 1)] = mixed.at[b][pl.ds(s, 8, stride=2), :]


VMEM = pl.BlockSpec(memory_space=pltpu.VMEM)
HBM = pl.BlockSpec(memory_space=pltpu.HBM)


def call(kernel, outs, operands, specs, scratch=()):
    return pl.pallas_call(
        kernel,
        out_shape=outs,
        in_specs=specs,
        out_specs=jax.tree.map(lambda _: VMEM, outs),
        scratch_shapes=list(scratch),
        compiler_params=pltpu.CompilerParams(vmem_limit_bytes=32 << 20),
        interpret=INTERPRET,
    )(*operands)


def whiten(spectra, owners, source_slots):
    return call(
        whiten_kernel,
        (
            jax.ShapeDtypeStruct((N_RECV, PAIRS * RECV_DEV, 128), bf16),
            jax.ShapeDtypeStruct((80, 256), bf16),
        ),
        [pltpu.with_memory_space_constraint(a, pltpu.HBM) for a in (spectra, owners, source_slots)],
        [HBM] * 3,
        [
            pltpu.VMEM((2, WIN, RECV_DEV, F), bf16),
            pltpu.SMEM((4,), jnp.int32),
            pltpu.SMEM((4, 8), jnp.int32),
            pltpu.VMEM((4, 2 * WIN * RECV_DEV, 128), f32),
            pltpu.VMEM((N_RECV * PAIRS * RECV_DEV, 128), f32),
            pltpu.VMEM((80, 256), f32),
            pltpu.SemaphoreType.DMA((CHUNKS + 2,)),
        ],
    )


def cross(pick, channels):
    return call(
        cross_kernel,
        jax.ShapeDtypeStruct((8, 64, 256), bf16),
        [pick, channels],
        [VMEM, VMEM],
        [pltpu.VMEM((2, N_TM * PITCH, 128), f32)],
    )


def gather(partial):
    return call(
        gather_kernel,
        jax.ShapeDtypeStruct((2 * N_RECV, 2, 128), f32),
        [partial],
        [VMEM],
        [pltpu.VMEM((256, 128), f32)],
    )


def lags(dofs):
    return call(
        lags_kernel,
        jax.ShapeDtypeStruct((2, RECV_DEV, F), f32),
        [dofs, *transform_table()],
        [VMEM] * 3,
        [pltpu.VMEM((128, 128), f32), pltpu.VMEM((4, 16, 128), f32)],
    )


def per_device(spectra, owners, source_slots):
    exchange = functools.partial(lax.all_to_all, split_axis=0, concat_axis=0, tiled=True)
    mine, pick = whiten(spectra, owners, source_slots)
    channels = exchange(mine, RECV)
    partial = exchange(cross(pick, channels), ("x", "core"))
    return lags(exchange(gather(partial), ("y_hi", *RECV)))


def solution(mesh):
    names = (*RECV, *TM)
    fine = Mesh(mesh.devices.reshape([SIZES[n] for n in names]), names)
    in_specs = (P(None, TM, RECV, None), P(), P())
    out_specs = P(TM, RECV, None)
    return jax.shard_map(
        per_device, mesh=fine, in_specs=in_specs, out_specs=out_specs, check_vma=False
    )
```

```python
import functools

import jax
import jax.numpy as jnp
import ml_dtypes
import numpy as np
from jax import lax
from jax.experimental import pallas as pl
from jax.experimental.pallas import tpu as pltpu
from jax.sharding import Mesh
from jax.sharding import PartitionSpec as P

F = 512
HALF = 64
N_RECV = 32
N_TM = 16
RECV_DEV = 8
WIN = 32
PAIRS = 8
EPSILON = 1e-05
PITCH = 40
INTERPRET = False

RECV = ("z", "y_lo")
ORDER = ('y_lo', 'z')
TM = ("x", "y_hi", "core")
SIZES = {"z": 8, "y_lo": 4, "x": 4, "y_hi": 2, "core": 2}

f32 = jnp.float32
bf16 = jnp.bfloat16


def transform_table():
    lag = np.arange(F)
    wave = np.zeros((2, PAIRS, N_RECV, F))
    for j in range(N_RECV):
        for p in range(PAIRS):
            f = PAIRS * j + p
            angle = 2 * np.pi * ((f * lag) % F) / F
            if f == 0:
                wave[0, p, j] = 1.0
                wave[1, p, j] = 1.0 - 2.0 * (lag % 2)
            else:
                wave[0, p, j] = np.cos(angle)
                wave[1, p, j] = -np.sin(angle)
    wave = (wave / F).reshape(F // 8, 8, F)
    high = wave.astype(ml_dtypes.bfloat16)
    low = (wave - high.astype(np.float64)).astype(ml_dtypes.bfloat16)
    return jnp.asarray(np.concatenate([high, low], axis=0))


def dot(a, b):
    return lax.dot_general(a, b, (((1,), (0,)), ((), ())), preferred_element_type=f32)


def dot_nt(a, b):
    return lax.dot_general(a, b, (((1,), (1,)), ((), ())), preferred_element_type=f32)


def iota(shape, dim):
    return lax.broadcasted_iota(jnp.int32, shape, dim)


def ones_where(mask):
    return jnp.where(mask, 1.0, 0.0).astype(bf16)


def tm_place(t):
    return (t % 2) * 8 + (t // 4) * 2 + (t // 2) % 2


def band():
    gap = iota((128, 128), 0) - iota((128, 128), 1)
    inside = ones_where(jnp.abs(gap) <= HALF)
    above = ones_where(gap >= HALF)
    below = ones_where(gap <= -HALF)
    nothing = jnp.zeros((128, 128), bf16)
    pieces = {0: inside, 1: above, -1: below}
    rows = [
        jnp.concatenate([pieces.get(b - a, nothing) for b in range(4)], axis=1) for a in range(4)
    ]
    return jnp.concatenate(rows, axis=0)


def source_picker(owners_ref, slots_ref, pick_ref):
    sub = iota((8, 128), 0)
    lane = iota((8, 128), 1)
    for odd in range(2):
        for half in range(2):
            key = jnp.zeros((8, 128), jnp.int32)
            for t in range(N_TM):
                place = tm_place(t)
                if place // 8 != half:
                    continue
                s = 2 * t + odd
                owner = owners_ref[s // 8]
                device = (owner % 4) * 8 + owner // 4
                channel = device * RECV_DEV + slots_ref[s // 8, s % 8]
                key = jnp.where(sub == place % 8, channel, key)
            found = jnp.concatenate(
                [jnp.where(key == lane, 1.0, 0.0), jnp.where(key == lane + 128, 1.0, 0.0)], axis=1
            )
            for dof in range(2):
                row = (2 * odd + dof) * N_TM + 8 * half
                pick_ref[row : row + 8, :] = found


def whiten_kernel(
    x_hbm, owners_hbm, slots_hbm, y_ref, pick_ref, x_ref, owners_ref, slots_ref, white, pick, sems
):
    is_first = lax.axis_index(ORDER) == 0
    copies = [pltpu.make_async_copy(x_hbm.at[c], x_ref.at[c], sems.at[c]) for c in range(2)]
    small = [
        pltpu.make_async_copy(owners_hbm, owners_ref, sems.at[2]),
        pltpu.make_async_copy(slots_hbm, slots_ref, sems.at[3]),
    ]
    for copy in copies + small:
        copy.start()

    near = band()
    bins = iota((8, F), 1)
    counts = (jnp.minimum(bins + HALF, F - 1) - jnp.maximum(bins - HALF, 0) + 1).astype(f32)
    share = (1.0 / counts)[:1]
    row = iota((256, 256), 0)
    column = iota((256, 256), 1)
    forward = ones_where(row == column)
    backward = ones_where((row + column) % 256 == 0)
    low = iota((256, 128), 1) < 64

    for copy in copies:
        copy.wait()
    re, im = [x_ref[c].astype(f32).reshape(WIN * RECV_DEV, F) for c in range(2)]
    energy = re * re + im * im
    first = energy.astype(bf16)
    second = (energy - first.astype(f32)).astype(bf16)
    total = dot(first, near) + dot(second, near)
    scale = lax.rsqrt(total * share + EPSILON)
    for c, value in enumerate((re, im)):
        scaled = value * scale
        here = slice(c * WIN * RECV_DEV, (c + 1) * WIN * RECV_DEV)
        for b in range(4):
            white.at[b][here, :] = scaled[:, 128 * b : 128 * (b + 1)]

    for copy in small:
        copy.wait()
    source_picker(owners_ref, slots_ref, pick)
    pick[64:80, :] = jnp.full((16, 256), jnp.where(is_first, 1.0, 0.0), f32)
    pick_ref[...] = pick[...].astype(bf16)

    def by_channel(b):
        strips = [white.at[b][pl.ds(r, 2 * WIN, stride=RECV_DEV), :] for r in range(RECV_DEV)]
        return jnp.concatenate(strips, axis=0).astype(bf16)

    blocks = [by_channel(b) for b in range(4)]
    ahead = dot_nt(forward, jnp.concatenate(blocks[:2], axis=1))
    behind = dot_nt(backward, jnp.concatenate(blocks[2:], axis=1))
    for g in range(4):
        one = ahead[:, 128 * g : 128 * (g + 1)]
        two = behind[:, 128 * g : 128 * (g + 1)]
        even = jnp.where(low, one, pltpu.roll(two, 64, 1)).reshape(N_RECV, 8, 128)
        odd = jnp.where(low, pltpu.roll(one, 64, 1), two).reshape(N_RECV, 8, 128)
        y_ref[:, 16 * g : 16 * (g + 1), :] = jnp.concatenate([even, odd], axis=1).astype(bf16)


def cross_kernel(pick_ref, y_ref, z_ref, wide, tall):
    tall[...] = y_ref[...].astype(f32).reshape(tall.shape)
    pick = pick_ref[:64, :]
    is_first = pick_ref[64:80, :128].astype(f32)[:1] > 0.5
    lane = iota((N_TM, 128), 1)
    real_lane = (lane // 32) % 2 == 0
    ahead = lane < 64
    sign = jnp.where(real_lane == ahead, -1.0, 1.0)
    nothing = jnp.zeros((64, 128), f32)
    for pair in range(PAIRS // 2):
        side = jnp.concatenate(
            [tall[pl.ds(2 * pair + i, 256, stride=8), :] for i in range(2)], axis=1
        ).astype(bf16)
        found = dot(pick, side)
        lefts = []
        for i in range(2):
            strips = []
            for q in range(4):
                strip = found[N_TM * q : N_TM * (q + 1), 128 * i : 128 * (i + 1)]
                first_bin = jnp.where(ahead == (q % 2 == 0), strip, 0.0)
                if q % 2:
                    strip = sign * jnp.where(
                        real_lane, pltpu.roll(strip, 96, 1), pltpu.roll(strip, 32, 1)
                    )
                if pair == 0 and i == 0:
                    strip = jnp.where(is_first, first_bin, strip)
                strips.append(strip)
            lefts.append(jnp.concatenate(strips, axis=0))
        left = jnp.concatenate(
            [
                jnp.concatenate([lefts[0], nothing], axis=1),
                jnp.concatenate([nothing, lefts[1]], axis=1),
            ],
            axis=0,
        )
        out = dot_nt(left.astype(bf16), side)
        for i in range(2):
            for q in range(4):
                row = 64 * i + N_TM * q
                for h in range(2):
                    wide.at[h][pl.ds(8 * q + 2 * pair + i, N_TM, stride=PITCH), :] = out[
                        row : row + N_TM, 128 * h : 128 * (h + 1)
                    ]
    for h in range(2):
        block = wide[h].reshape(N_TM, PITCH, 128)[:, :32, :]
        z_ref[:, :, 128 * h : 128 * (h + 1)] = block.astype(bf16).reshape(8, 64, 128)


def gather_kernel(z_ref, q_ref, tall):
    total = jnp.sum(z_ref[...].astype(f32), axis=0)
    for h in range(2):
        block = total[:, 128 * h : 128 * (h + 1)]
        tall[128 * h : 128 * (h + 1), :] = jnp.concatenate([block, jnp.zeros_like(block)], axis=0).T
    group = iota((N_RECV, 128), 1) // 32
    for h in range(2):
        channels = [tall[pl.ds(4 * h + r, N_RECV, stride=8), :] for r in range(4)]
        for y in range(2):
            packed = jnp.zeros((N_RECV, 128), f32)
            for r in range(4):
                moved = channels[r]
                if r != y:
                    moved = pltpu.roll(moved, (32 * (r - y)) % 128, 1)
                packed = jnp.where(group == r, moved, packed)
            for o in range(4):
                row = 16 * o + 8 * y
                q_ref[row : row + 8, h, :] = packed[8 * o : 8 * (o + 1)]


def lags_kernel(q_ref, wave_ref, out_ref, turned, mixed):
    both = [q_ref[:, h, :].reshape(4, 2, 8, 128) for h in range(2)]
    sums = [(b[:, 0] + b[:, 1]).reshape(N_RECV, 128) for b in both]
    turned[...] = jnp.concatenate(sums + [jnp.zeros((64, 128), f32)], axis=0).T
    group = iota((8, 128), 1) // 32
    rows = [[], []]
    for q in range(4):
        tiles = [jnp.zeros((8, 128), f32) for _ in range(2)]
        for i in range(4):
            block = turned[pl.ds(4 * q + i, 8, stride=16), :]
            for h in range(2):
                moved = pltpu.roll(block, (32 * (i - h)) % 128, 1) if i != h else block
                tiles[h] = jnp.where(group == i, moved, tiles[h])
        for h in range(2):
            rows[h].append(tiles[h])
    value = jnp.concatenate([jnp.concatenate(r, axis=1) for r in rows], axis=0)
    first = value.astype(bf16)
    second = (value - first.astype(f32)).astype(bf16)
    high = wave_ref[: F // 8].reshape(F, F)
    low = wave_ref[F // 8 :].reshape(F, F)
    both = dot(jnp.concatenate([first, second], axis=0), high)
    lags = both[:16] + (both[16:] + dot(first, low))
    for b in range(4):
        mixed.at[b][...] = lags[:, 128 * b : 128 * (b + 1)]
    for s in range(2):
        for b in range(4):
            out_ref[s, :, 128 * b : 128 * (b + 1)] = mixed.at[b][pl.ds(s, 8, stride=2), :]


VMEM = pl.BlockSpec(memory_space=pltpu.VMEM)
HBM = pl.BlockSpec(memory_space=pltpu.HBM)


def call(kernel, outs, operands, specs, scratch=()):
    return pl.pallas_call(
        kernel,
        out_shape=outs,
        in_specs=specs,
        out_specs=jax.tree.map(lambda _: VMEM, outs),
        scratch_shapes=list(scratch),
        compiler_params=pltpu.CompilerParams(vmem_limit_bytes=32 << 20),
        interpret=INTERPRET,
    )(*operands)


def whiten(spectra, owners, source_slots):
    return call(
        whiten_kernel,
        (
            jax.ShapeDtypeStruct((N_RECV, PAIRS * RECV_DEV, 128), bf16),
            jax.ShapeDtypeStruct((80, 256), bf16),
        ),
        [pltpu.with_memory_space_constraint(a, pltpu.HBM) for a in (spectra, owners, source_slots)],
        [HBM] * 3,
        [
            pltpu.VMEM((2, WIN, RECV_DEV, F), bf16),
            pltpu.SMEM((4,), jnp.int32),
            pltpu.SMEM((4, 8), jnp.int32),
            pltpu.VMEM((4, 2 * WIN * RECV_DEV, 128), f32),
            pltpu.VMEM((80, 256), f32),
            pltpu.SemaphoreType.DMA((4,)),
        ],
    )


def cross(pick, channels):
    return call(
        cross_kernel,
        jax.ShapeDtypeStruct((8, 64, 256), bf16),
        [pick, channels],
        [VMEM, VMEM],
        [pltpu.VMEM((2, N_TM * PITCH, 128), f32), pltpu.VMEM((2048, 128), f32)],
    )


def gather(partial):
    return call(
        gather_kernel,
        jax.ShapeDtypeStruct((2 * N_RECV, 2, 128), f32),
        [partial],
        [VMEM],
        [pltpu.VMEM((256, 128), f32)],
    )


def lags(dofs):
    return call(
        lags_kernel,
        jax.ShapeDtypeStruct((2, RECV_DEV, F), f32),
        [dofs, transform_table()],
        [VMEM] * 2,
        [pltpu.VMEM((128, 128), f32), pltpu.VMEM((4, 16, 128), f32)],
    )


def per_device(spectra, owners, source_slots):
    exchange = functools.partial(lax.all_to_all, split_axis=0, concat_axis=0, tiled=True)
    mine, pick = whiten(spectra, owners, source_slots)
    channels = exchange(mine, ORDER)
    partial = exchange(cross(pick, channels), ('core', 'x'))
    return lags(exchange(gather(partial), ("y_lo", "y_hi", "z")))


def solution(mesh):
    names = (*RECV, *TM)
    fine = Mesh(mesh.devices.reshape([SIZES[n] for n in names]), names)
    in_specs = (P(None, TM, RECV, None), P(), P())
    out_specs = P(TM, RECV, None)
    return jax.shard_map(
        per_device, mesh=fine, in_specs=in_specs, out_specs=out_specs, check_vma=False
    )
```

```python
import functools

import jax
import jax.numpy as jnp
import ml_dtypes
import numpy as np
from jax import lax
from jax.experimental import pallas as pl
from jax.experimental.pallas import tpu as pltpu
from jax.sharding import Mesh
from jax.sharding import PartitionSpec as P

F = 512
HALF = 64
N_RECV = 32
N_TM = 16
RECV_DEV = 8
WIN = 32
PAIRS = 8
EPSILON = 1e-05
PITCH = 40
INTERPRET = False

RECV = ("z", "y_lo")
ORDER = ('y_lo', 'z')
TM = ("x", "y_hi", "core")
SIZES = {"z": 8, "y_lo": 4, "x": 4, "y_hi": 2, "core": 2}

f32 = jnp.float32
bf16 = jnp.bfloat16


def transform_table():
    lag = np.arange(F)
    wave = np.zeros((2, PAIRS, N_RECV, F))
    for j in range(N_RECV):
        for p in range(PAIRS):
            f = PAIRS * j + p
            angle = 2 * np.pi * ((f * lag) % F) / F
            if f == 0:
                wave[0, p, j] = 1.0
                wave[1, p, j] = 1.0 - 2.0 * (lag % 2)
            else:
                wave[0, p, j] = np.cos(angle)
                wave[1, p, j] = -np.sin(angle)
    wave = (wave / F).reshape(F // 8, 8, F)
    high = wave.astype(ml_dtypes.bfloat16)
    low = (wave - high.astype(np.float64)).astype(ml_dtypes.bfloat16)
    return jnp.asarray(np.concatenate([high, low], axis=0))


def dot(a, b):
    return lax.dot_general(a, b, (((1,), (0,)), ((), ())), preferred_element_type=f32)


def dot_nt(a, b):
    return lax.dot_general(a, b, (((1,), (1,)), ((), ())), preferred_element_type=f32)


def iota(shape, dim):
    return lax.broadcasted_iota(jnp.int32, shape, dim)


def ones_where(mask):
    return jnp.where(mask, 1.0, 0.0).astype(bf16)


def tm_place(t):
    return (t % 2) * 8 + (t // 4) * 2 + (t // 2) % 2


def band():
    gap = iota((128, 128), 0) - iota((128, 128), 1)
    inside = ones_where(jnp.abs(gap) <= HALF)
    above = ones_where(gap >= HALF)
    below = ones_where(gap <= -HALF)
    nothing = jnp.zeros((128, 128), bf16)
    pieces = {0: inside, 1: above, -1: below}
    rows = [
        jnp.concatenate([pieces.get(b - a, nothing) for b in range(4)], axis=1) for a in range(4)
    ]
    return jnp.concatenate(rows, axis=0)


def source_picker(owners_ref, slots_ref, pick_ref):
    sub = iota((8, 128), 0)
    lane = iota((8, 128), 1)
    for odd in range(2):
        for half in range(2):
            key = jnp.zeros((8, 128), jnp.int32)
            for t in range(N_TM):
                place = tm_place(t)
                if place // 8 != half:
                    continue
                s = 2 * t + odd
                owner = owners_ref[s // 8]
                device = (owner % 4) * 8 + owner // 4
                channel = device * RECV_DEV + slots_ref[s // 8, s % 8]
                key = jnp.where(sub == place % 8, channel, key)
            found = jnp.concatenate(
                [jnp.where(key == lane, 1.0, 0.0), jnp.where(key == lane + 128, 1.0, 0.0)], axis=1
            )
            for dof in range(2):
                row = (2 * odd + dof) * N_TM + 8 * half
                pick_ref[row : row + 8, :] = found


def whiten_kernel(
    x_hbm, owners_hbm, slots_hbm, y_ref, pick_ref, x_ref, owners_ref, slots_ref, white, pick, sems
):
    is_first = lax.axis_index(ORDER) == 0
    copies = [pltpu.make_async_copy(x_hbm.at[c], x_ref.at[c], sems.at[c]) for c in range(2)]
    small = [
        pltpu.make_async_copy(owners_hbm, owners_ref, sems.at[2]),
        pltpu.make_async_copy(slots_hbm, slots_ref, sems.at[3]),
    ]
    for copy in copies + small:
        copy.start()

    near = band()
    bins = iota((8, F), 1)
    counts = (jnp.minimum(bins + HALF, F - 1) - jnp.maximum(bins - HALF, 0) + 1).astype(f32)
    share = (1.0 / counts)[:1]
    row = iota((256, 256), 0)
    column = iota((256, 256), 1)
    forward = ones_where(row == column)
    backward = ones_where((row + column) % 256 == 0)
    low = iota((256, 128), 1) < 64

    for copy in copies:
        copy.wait()
    re, im = [x_ref[c].astype(f32).reshape(WIN * RECV_DEV, F) for c in range(2)]
    energy = re * re + im * im
    first = energy.astype(bf16)
    second = (energy - first.astype(f32)).astype(bf16)
    total = dot(first, near) + dot(second, near)
    scale = lax.rsqrt(total * share + EPSILON)
    for c, value in enumerate((re, im)):
        scaled = value * scale
        here = slice(c * WIN * RECV_DEV, (c + 1) * WIN * RECV_DEV)
        for b in range(4):
            white.at[b][here, :] = scaled[:, 128 * b : 128 * (b + 1)]

    for copy in small:
        copy.wait()
    source_picker(owners_ref, slots_ref, pick)
    pick[64:80, :] = jnp.full((16, 256), jnp.where(is_first, 1.0, 0.0), f32)
    pick_ref[...] = pick[...].astype(bf16)

    def by_channel(b):
        strips = [white.at[b][pl.ds(r, 2 * WIN, stride=RECV_DEV), :] for r in range(RECV_DEV)]
        return jnp.concatenate(strips, axis=0).astype(bf16)

    blocks = [by_channel(b) for b in range(4)]
    ahead = dot_nt(forward, jnp.concatenate(blocks[:2], axis=1))
    behind = dot_nt(backward, jnp.concatenate(blocks[2:], axis=1))
    for g in range(4):
        one = ahead[:, 128 * g : 128 * (g + 1)]
        two = behind[:, 128 * g : 128 * (g + 1)]
        even = jnp.where(low, one, pltpu.roll(two, 64, 1)).reshape(N_RECV, 8, 128)
        odd = jnp.where(low, pltpu.roll(one, 64, 1), two).reshape(N_RECV, 8, 128)
        y_ref[:, 16 * g : 16 * (g + 1), :] = jnp.concatenate([even, odd], axis=1).astype(bf16)


def cross_kernel(pick_ref, y_ref, z_ref, wide, tall):
    rows = N_RECV * PAIRS * RECV_DEV
    tall[:rows, :] = y_ref[...].astype(f32).reshape(rows, 128)
    pick = pick_ref[:64, :]
    is_first = pick_ref[64:80, :128].astype(f32)[:1] > 0.5
    lane = iota((N_TM, 128), 1)
    real_lane = (lane // 32) % 2 == 0
    ahead = lane < 64
    sign = jnp.where(real_lane == ahead, -1.0, 1.0)
    nothing = jnp.zeros((64, 128), f32)
    for pair in range(PAIRS // 2):
        side = jnp.concatenate(
            [tall[pl.ds(2 * pair + i, 256, stride=8), :] for i in range(2)], axis=1
        ).astype(bf16)
        found = dot(pick, side)
        lefts = []
        for i in range(2):
            strips = []
            for q in range(4):
                strip = found[N_TM * q : N_TM * (q + 1), 128 * i : 128 * (i + 1)]
                first_bin = jnp.where(ahead == (q % 2 == 0), strip, 0.0)
                if q % 2:
                    strip = sign * jnp.where(
                        real_lane, pltpu.roll(strip, 96, 1), pltpu.roll(strip, 32, 1)
                    )
                if pair == 0 and i == 0:
                    strip = jnp.where(is_first, first_bin, strip)
                strips.append(strip)
            lefts.append(jnp.concatenate(strips, axis=0))
        left = jnp.concatenate(
            [
                jnp.concatenate([lefts[0], nothing], axis=1),
                jnp.concatenate([nothing, lefts[1]], axis=1),
            ],
            axis=0,
        )
        out = dot_nt(left.astype(bf16), side)
        for i in range(2):
            for q in range(4):
                row = 64 * i + N_TM * q
                for h in range(2):
                    wide.at[h][pl.ds(8 * q + 2 * pair + i, N_TM, stride=PITCH), :] = out[
                        row : row + N_TM, 128 * h : 128 * (h + 1)
                    ]
    for h in range(2):
        block = wide[h, : N_TM * PITCH, :].reshape(N_TM, PITCH, 128)[:, :32, :]
        z_ref[:, :, 128 * h : 128 * (h + 1)] = block.astype(bf16).reshape(8, 64, 128)


def gather_kernel(z_ref, q_ref, tall):
    total = jnp.sum(z_ref[...].astype(f32), axis=0)
    for h in range(2):
        block = total[:, 128 * h : 128 * (h + 1)]
        tall[128 * h : 128 * (h + 1), :] = jnp.concatenate([block, jnp.zeros_like(block)], axis=0).T
    group = iota((N_RECV, 128), 1) // 32
    for h in range(2):
        channels = [tall[pl.ds(4 * h + r, N_RECV, stride=8), :] for r in range(4)]
        for y in range(2):
            packed = jnp.zeros((N_RECV, 128), f32)
            for r in range(4):
                moved = channels[r]
                if r != y:
                    moved = pltpu.roll(moved, (32 * (r - y)) % 128, 1)
                packed = jnp.where(group == r, moved, packed)
            for o in range(4):
                row = 16 * o + 8 * y
                q_ref[row : row + 8, h, :] = packed[8 * o : 8 * (o + 1)]


def lags_kernel(q_ref, wave_ref, out_ref, turned, mixed):
    both = [q_ref[:, h, :].reshape(4, 2, 8, 128) for h in range(2)]
    sums = [(b[:, 0] + b[:, 1]).reshape(N_RECV, 128) for b in both]
    turned[:128, :] = jnp.concatenate(sums + [jnp.zeros((64, 128), f32)], axis=0).T
    group = iota((8, 128), 1) // 32
    rows = [[], []]
    for q in range(4):
        tiles = [jnp.zeros((8, 128), f32) for _ in range(2)]
        for i in range(4):
            block = turned[pl.ds(4 * q + i, 8, stride=16), :]
            for h in range(2):
                moved = pltpu.roll(block, (32 * (i - h)) % 128, 1) if i != h else block
                tiles[h] = jnp.where(group == i, moved, tiles[h])
        for h in range(2):
            rows[h].append(tiles[h])
    value = jnp.concatenate([jnp.concatenate(r, axis=1) for r in rows], axis=0)
    first = value.astype(bf16)
    second = (value - first.astype(f32)).astype(bf16)
    high = wave_ref[: F // 8].reshape(F, F)
    low = wave_ref[F // 8 :].reshape(F, F)
    both = dot(jnp.concatenate([first, second], axis=0), high)
    lags = both[:16] + (both[16:] + dot(first, low))
    for b in range(4):
        mixed.at[b][:16, :] = lags[:, 128 * b : 128 * (b + 1)]
    for s in range(2):
        for b in range(4):
            out_ref[s, :, 128 * b : 128 * (b + 1)] = mixed.at[b][pl.ds(s, 8, stride=2), :]


VMEM = pl.BlockSpec(memory_space=pltpu.VMEM)
HBM = pl.BlockSpec(memory_space=pltpu.HBM)


def call(kernel, outs, operands, specs, scratch=()):
    return pl.pallas_call(
        kernel,
        out_shape=outs,
        in_specs=specs,
        out_specs=jax.tree.map(lambda _: VMEM, outs),
        scratch_shapes=list(scratch),
        compiler_params=pltpu.CompilerParams(vmem_limit_bytes=32 << 20),
        interpret=INTERPRET,
    )(*operands)


def whiten(spectra, owners, source_slots):
    return call(
        whiten_kernel,
        (
            jax.ShapeDtypeStruct((N_RECV, PAIRS * RECV_DEV, 128), bf16),
            jax.ShapeDtypeStruct((80, 256), bf16),
        ),
        [pltpu.with_memory_space_constraint(a, pltpu.HBM) for a in (spectra, owners, source_slots)],
        [HBM] * 3,
        [
            pltpu.VMEM((2, WIN, RECV_DEV, F), bf16),
            pltpu.SMEM((4,), jnp.int32),
            pltpu.SMEM((4, 8), jnp.int32),
            pltpu.VMEM((4, 2 * WIN * RECV_DEV + 8, 128), f32),
            pltpu.VMEM((80, 256), f32),
            pltpu.SemaphoreType.DMA((4,)),
        ],
    )


def cross(pick, channels):
    return call(
        cross_kernel,
        jax.ShapeDtypeStruct((8, 64, 256), bf16),
        [pick, channels],
        [VMEM, VMEM],
        [
            pltpu.VMEM((2, (N_TM + 1) * PITCH, 128), f32),
            pltpu.VMEM((N_RECV * PAIRS * RECV_DEV + 8, 128), f32),
        ],
    )


def gather(partial):
    return call(
        gather_kernel,
        jax.ShapeDtypeStruct((2 * N_RECV, 2, 128), f32),
        [partial],
        [VMEM],
        [pltpu.VMEM((256 + 8, 128), f32)],
    )


def lags(dofs):
    return call(
        lags_kernel,
        jax.ShapeDtypeStruct((2, RECV_DEV, F), f32),
        [dofs, transform_table()],
        [VMEM] * 2,
        [pltpu.VMEM((128 + 16, 128), f32), pltpu.VMEM((4, 16 + 8, 128), f32)],
    )


def per_device(spectra, owners, source_slots):
    exchange = functools.partial(lax.all_to_all, split_axis=0, concat_axis=0, tiled=True)
    mine, pick = whiten(spectra, owners, source_slots)
    channels = exchange(mine, ORDER)
    partial = exchange(cross(pick, channels), ('core', 'x'))
    return lags(exchange(gather(partial), ("y_lo", "y_hi", "z")))


def solution(mesh):
    names = (*RECV, *TM)
    fine = Mesh(mesh.devices.reshape([SIZES[n] for n in names]), names)
    in_specs = (P(None, TM, RECV, None), P(), P())
    out_specs = P(TM, RECV, None)
    return jax.shard_map(
        per_device, mesh=fine, in_specs=in_specs, out_specs=out_specs, check_vma=False
    )
```

```python
import functools

import jax
import jax.numpy as jnp
import ml_dtypes
import numpy as np
from jax import lax
from jax.experimental import pallas as pl
from jax.experimental.pallas import tpu as pltpu
from jax.sharding import Mesh
from jax.sharding import PartitionSpec as P

F = 512
HALF = 64
N_RECV = 32
N_TM = 16
RECV_DEV = 8
WIN = 32
PAIRS = 8
EPSILON = 1e-05
PITCH = 40
INTERPRET = False

RECV = ("z", "y_lo")
ORDER = ('y_lo', 'z')
TM = ("x", "y_hi", "core")
SIZES = {"z": 8, "y_lo": 4, "x": 4, "y_hi": 2, "core": 2}

f32 = jnp.float32
bf16 = jnp.bfloat16


def transform_table():
    lag = np.arange(F)
    wave = np.zeros((2, PAIRS, N_RECV, F))
    for j in range(N_RECV):
        for p in range(PAIRS):
            f = PAIRS * j + p
            angle = 2 * np.pi * ((f * lag) % F) / F
            if f == 0:
                wave[0, p, j] = 1.0
                wave[1, p, j] = 1.0 - 2.0 * (lag % 2)
            else:
                wave[0, p, j] = np.cos(angle)
                wave[1, p, j] = -np.sin(angle)
    wave = (wave / F).reshape(F // 8, 8, F)
    high = wave.astype(ml_dtypes.bfloat16)
    low = (wave - high.astype(np.float64)).astype(ml_dtypes.bfloat16)
    return jnp.asarray(np.concatenate([high, low], axis=0))


def dot(a, b):
    return lax.dot_general(a, b, (((1,), (0,)), ((), ())), preferred_element_type=f32)


def dot_nt(a, b):
    return lax.dot_general(a, b, (((1,), (1,)), ((), ())), preferred_element_type=f32)


def iota(shape, dim):
    return lax.broadcasted_iota(jnp.int32, shape, dim)


def ones_where(mask):
    return jnp.where(mask, 1.0, 0.0).astype(bf16)


def tm_place(t):
    return (t % 2) * 8 + (t // 4) * 2 + (t // 2) % 2


def band():
    gap = iota((128, 128), 0) - iota((128, 128), 1)
    inside = ones_where(jnp.abs(gap) <= HALF)
    above = ones_where(gap >= HALF)
    below = ones_where(gap <= -HALF)
    nothing = jnp.zeros((128, 128), bf16)
    pieces = {0: inside, 1: above, -1: below}
    rows = [
        jnp.concatenate([pieces.get(b - a, nothing) for b in range(4)], axis=1) for a in range(4)
    ]
    return jnp.concatenate(rows, axis=0)


def source_picker(owners_ref, slots_ref, pick_ref):
    sub = iota((8, 128), 0)
    lane = iota((8, 128), 1)
    for odd in range(2):
        for half in range(2):
            key = jnp.zeros((8, 128), jnp.int32)
            for t in range(N_TM):
                place = tm_place(t)
                if place // 8 != half:
                    continue
                s = 2 * t + odd
                owner = owners_ref[s // 8]
                device = (owner % 4) * 8 + owner // 4
                channel = device * RECV_DEV + slots_ref[s // 8, s % 8]
                key = jnp.where(sub == place % 8, channel, key)
            found = jnp.concatenate(
                [jnp.where(key == lane, 1.0, 0.0), jnp.where(key == lane + 128, 1.0, 0.0)], axis=1
            )
            for dof in range(2):
                row = (2 * odd + dof) * N_TM + 8 * half
                pick_ref[row : row + 8, :] = found


def whiten_kernel(
    x_hbm, owners_hbm, slots_hbm, y_ref, pick_ref, x_ref, owners_ref, slots_ref, white, pick, sems
):
    is_first = lax.axis_index(ORDER) == 0
    copies = [pltpu.make_async_copy(x_hbm.at[c], x_ref.at[c], sems.at[c]) for c in range(2)]
    small = [
        pltpu.make_async_copy(owners_hbm, owners_ref, sems.at[2]),
        pltpu.make_async_copy(slots_hbm, slots_ref, sems.at[3]),
    ]
    for copy in copies + small:
        copy.start()

    near = band()
    bins = iota((8, F), 1)
    counts = (jnp.minimum(bins + HALF, F - 1) - jnp.maximum(bins - HALF, 0) + 1).astype(f32)
    share = (1.0 / counts)[:1]
    row = iota((256, 256), 0)
    column = iota((256, 256), 1)
    forward = ones_where(row == column)
    backward = ones_where((row + column) % 256 == 0)
    low = iota((256, 128), 1) < 64

    copies[0].wait()
    re = x_ref[0].astype(f32).reshape(WIN * RECV_DEV, F)
    energy = re * re
    copies[1].wait()
    im = x_ref[1].astype(f32).reshape(WIN * RECV_DEV, F)
    energy = energy + im * im
    first = energy.astype(bf16)
    second = (energy - first.astype(f32)).astype(bf16)
    total = dot(first, near) + dot(second, near)
    scale = lax.rsqrt(total * share + EPSILON)
    for c, value in enumerate((re, im)):
        scaled = value * scale
        here = slice(c * WIN * RECV_DEV, (c + 1) * WIN * RECV_DEV)
        for b in range(4):
            white.at[b][here, :] = scaled[:, 128 * b : 128 * (b + 1)]

    for copy in small:
        copy.wait()
    source_picker(owners_ref, slots_ref, pick)
    pick[64:80, :] = jnp.full((16, 256), jnp.where(is_first, 1.0, 0.0), f32)
    pick_ref[...] = pick[...].astype(bf16)

    def by_channel(b):
        strips = [white.at[b][pl.ds(r, 2 * WIN, stride=RECV_DEV), :] for r in range(RECV_DEV)]
        return jnp.concatenate(strips, axis=0).astype(bf16)

    blocks = [by_channel(b) for b in range(4)]
    ahead = dot_nt(forward, jnp.concatenate(blocks[:2], axis=1))
    behind = dot_nt(backward, jnp.concatenate(blocks[2:], axis=1))
    for g in range(4):
        one = ahead[:, 128 * g : 128 * (g + 1)]
        two = behind[:, 128 * g : 128 * (g + 1)]
        even = jnp.where(low, one, pltpu.roll(two, 64, 1)).reshape(N_RECV, 8, 128)
        odd = jnp.where(low, pltpu.roll(one, 64, 1), two).reshape(N_RECV, 8, 128)
        y_ref[:, 16 * g : 16 * (g + 1), :] = jnp.concatenate([even, odd], axis=1).astype(bf16)


def cross_kernel(pick_ref, y_ref, z_ref, wide, tall):
    rows = N_RECV * PAIRS * RECV_DEV
    tall[:rows, :] = y_ref[...].astype(f32).reshape(rows, 128)
    pick = pick_ref[:64, :]
    is_first = pick_ref[64:80, :128].astype(f32)[:1] > 0.5
    lane = iota((N_TM, 128), 1)
    real_lane = (lane // 32) % 2 == 0
    ahead = lane < 64
    sign = jnp.where(real_lane == ahead, -1.0, 1.0)
    nothing = jnp.zeros((64, 128), f32)
    sides = [
        jnp.concatenate(
            [tall[pl.ds(2 * pair + i, 256, stride=8), :] for i in range(2)], axis=1
        ).astype(bf16)
        for pair in range(PAIRS // 2)
    ]
    every = dot(pick, jnp.concatenate(sides, axis=1))
    for pair, side in enumerate(sides):
        found = every[:, 256 * pair : 256 * (pair + 1)]
        lefts = []
        for i in range(2):
            strips = []
            for q in range(4):
                strip = found[N_TM * q : N_TM * (q + 1), 128 * i : 128 * (i + 1)]
                first_bin = jnp.where(ahead == (q % 2 == 0), strip, 0.0)
                if q % 2:
                    strip = sign * jnp.where(
                        real_lane, pltpu.roll(strip, 96, 1), pltpu.roll(strip, 32, 1)
                    )
                if pair == 0 and i == 0:
                    strip = jnp.where(is_first, first_bin, strip)
                strips.append(strip)
            lefts.append(jnp.concatenate(strips, axis=0))
        left = jnp.concatenate(
            [
                jnp.concatenate([lefts[0], nothing], axis=1),
                jnp.concatenate([nothing, lefts[1]], axis=1),
            ],
            axis=0,
        )
        out = dot_nt(left.astype(bf16), side)
        for i in range(2):
            for q in range(4):
                row = 64 * i + N_TM * q
                for h in range(2):
                    wide.at[h][pl.ds(8 * q + 2 * pair + i, N_TM, stride=PITCH), :] = out[
                        row : row + N_TM, 128 * h : 128 * (h + 1)
                    ]
    for h in range(2):
        block = wide[h, : N_TM * PITCH, :].reshape(N_TM, PITCH, 128)[:, :32, :]
        z_ref[:, :, 128 * h : 128 * (h + 1)] = block.astype(bf16).reshape(8, 64, 128)


def gather_kernel(z_ref, q_ref, tall):
    total = jnp.sum(z_ref[...].astype(f32), axis=0)
    for h in range(2):
        tall[128 * h : 128 * (h + 1), :64] = total[:, 128 * h : 128 * (h + 1)].T
    group = iota((N_RECV, 128), 1) // 32
    for h in range(2):
        channels = [tall[pl.ds(4 * h + r, N_RECV, stride=8), :] for r in range(4)]
        for y in range(2):
            packed = jnp.zeros((N_RECV, 128), f32)
            for r in range(4):
                moved = channels[r]
                if r != y:
                    moved = pltpu.roll(moved, (32 * (r - y)) % 128, 1)
                packed = jnp.where(group == r, moved, packed)
            for o in range(4):
                row = 16 * o + 8 * y
                q_ref[row : row + 8, h, :] = packed[8 * o : 8 * (o + 1)]


def lags_kernel(q_ref, wave_ref, out_ref, turned, mixed):
    both = [q_ref[:, h, :].reshape(4, 2, 8, 128) for h in range(2)]
    sums = [(b[:, 0] + b[:, 1]).reshape(N_RECV, 128) for b in both]
    turned[:128, :64] = jnp.concatenate(sums, axis=0).T
    group = iota((8, 128), 1) // 32
    rows = [[], []]
    for q in range(4):
        tiles = [jnp.zeros((8, 128), f32) for _ in range(2)]
        for i in range(4):
            block = turned[pl.ds(4 * q + i, 8, stride=16), :]
            for h in range(2):
                moved = pltpu.roll(block, (32 * (i - h)) % 128, 1) if i != h else block
                tiles[h] = jnp.where(group == i, moved, tiles[h])
        for h in range(2):
            rows[h].append(tiles[h])
    value = jnp.concatenate([jnp.concatenate(r, axis=1) for r in rows], axis=0)
    first = value.astype(bf16)
    second = (value - first.astype(f32)).astype(bf16)
    high = wave_ref[: F // 8].reshape(F, F)
    low = wave_ref[F // 8 :].reshape(F, F)
    both = dot(jnp.concatenate([first, second], axis=0), high)
    lags = both[:16] + (both[16:] + dot(first, low))
    for b in range(4):
        mixed.at[b][:16, :] = lags[:, 128 * b : 128 * (b + 1)]
    for s in range(2):
        for b in range(4):
            out_ref[s, :, 128 * b : 128 * (b + 1)] = mixed.at[b][pl.ds(s, 8, stride=2), :]


VMEM = pl.BlockSpec(memory_space=pltpu.VMEM)
HBM = pl.BlockSpec(memory_space=pltpu.HBM)


def call(kernel, outs, operands, specs, scratch=()):
    return pl.pallas_call(
        kernel,
        out_shape=outs,
        in_specs=specs,
        out_specs=jax.tree.map(lambda _: VMEM, outs),
        scratch_shapes=list(scratch),
        compiler_params=pltpu.CompilerParams(vmem_limit_bytes=32 << 20),
        interpret=INTERPRET,
    )(*operands)


def whiten(spectra, owners, source_slots):
    return call(
        whiten_kernel,
        (
            jax.ShapeDtypeStruct((N_RECV, PAIRS * RECV_DEV, 128), bf16),
            jax.ShapeDtypeStruct((80, 256), bf16),
        ),
        [pltpu.with_memory_space_constraint(a, pltpu.HBM) for a in (spectra, owners, source_slots)],
        [HBM] * 3,
        [
            pltpu.VMEM((2, WIN, RECV_DEV, F), bf16),
            pltpu.SMEM((4,), jnp.int32),
            pltpu.SMEM((4, 8), jnp.int32),
            pltpu.VMEM((4, 2 * WIN * RECV_DEV + 8, 128), f32),
            pltpu.VMEM((80, 256), f32),
            pltpu.SemaphoreType.DMA((4,)),
        ],
    )


def cross(pick, channels):
    return call(
        cross_kernel,
        jax.ShapeDtypeStruct((8, 64, 256), bf16),
        [pick, channels],
        [VMEM, VMEM],
        [
            pltpu.VMEM((2, (N_TM + 1) * PITCH, 128), f32),
            pltpu.VMEM((N_RECV * PAIRS * RECV_DEV + 8, 128), f32),
        ],
    )


def gather(partial):
    return call(
        gather_kernel,
        jax.ShapeDtypeStruct((2 * N_RECV, 2, 128), f32),
        [partial],
        [VMEM],
        [pltpu.VMEM((256 + 8, 128), f32)],
    )


def lags(dofs):
    return call(
        lags_kernel,
        jax.ShapeDtypeStruct((2, RECV_DEV, F), f32),
        [dofs, transform_table()],
        [VMEM] * 2,
        [pltpu.VMEM((128 + 16, 128), f32), pltpu.VMEM((4, 16 + 8, 128), f32)],
    )


def per_device(spectra, owners, source_slots):
    exchange = functools.partial(lax.all_to_all, split_axis=0, concat_axis=0, tiled=True)
    mine, pick = whiten(spectra, owners, source_slots)
    channels = exchange(mine, ORDER)
    partial = exchange(cross(pick, channels), ('core', 'x'))
    return lags(exchange(gather(partial), ("y_lo", "y_hi", "z")))


def solution(mesh):
    names = (*RECV, *TM)
    fine = Mesh(mesh.devices.reshape([SIZES[n] for n in names]), names)
    in_specs = (P(None, TM, RECV, None), P(), P())
    out_specs = P(TM, RECV, None)
    return jax.shard_map(
        per_device, mesh=fine, in_specs=in_specs, out_specs=out_specs, check_vma=False
    )
```

```python
import functools

import jax
import jax.numpy as jnp
import ml_dtypes
import numpy as np
from jax import lax
from jax.experimental import pallas as pl
from jax.experimental.pallas import tpu as pltpu
from jax.sharding import Mesh
from jax.sharding import PartitionSpec as P

F = 512
HALF = 64
N_RECV = 32
N_TM = 16
RECV_DEV = 8
WIN = 32
PAIRS = 8
EPSILON = 1e-05
PITCH = 40
INTERPRET = False

RECV = ("z", "y_lo")
ORDER = ('y_lo', 'z')
TM = ("x", "y_hi", "core")
SIZES = {"z": 8, "y_lo": 4, "x": 4, "y_hi": 2, "core": 2}

f32 = jnp.float32
bf16 = jnp.bfloat16


def transform_table():
    lag = np.arange(F)
    wave = np.zeros((2, PAIRS, N_RECV, F))
    for j in range(N_RECV):
        for p in range(PAIRS):
            f = PAIRS * j + p
            angle = 2 * np.pi * ((f * lag) % F) / F
            if f == 0:
                wave[0, p, j] = 1.0
                wave[1, p, j] = 1.0 - 2.0 * (lag % 2)
            else:
                wave[0, p, j] = np.cos(angle)
                wave[1, p, j] = -np.sin(angle)
    wave = (wave / F).reshape(F // 8, 8, F)
    high = wave.astype(ml_dtypes.bfloat16)
    low = (wave - high.astype(np.float64)).astype(ml_dtypes.bfloat16)
    return jnp.asarray(np.concatenate([high, low], axis=0))


def dot(a, b):
    return lax.dot_general(a, b, (((1,), (0,)), ((), ())), preferred_element_type=f32)


def dot_nt(a, b):
    return lax.dot_general(a, b, (((1,), (1,)), ((), ())), preferred_element_type=f32)


def iota(shape, dim):
    return lax.broadcasted_iota(jnp.int32, shape, dim)


def ones_where(mask):
    return jnp.where(mask, 1.0, 0.0).astype(bf16)


def tm_place(t):
    return (t % 2) * 8 + (t // 4) * 2 + (t // 2) % 2


def band():
    gap = iota((128, 128), 0) - iota((128, 128), 1)
    inside = ones_where(jnp.abs(gap) <= HALF)
    above = ones_where(gap >= HALF)
    below = ones_where(gap <= -HALF)
    nothing = jnp.zeros((128, 128), bf16)
    pieces = {0: inside, 1: above, -1: below}
    rows = [
        jnp.concatenate([pieces.get(b - a, nothing) for b in range(4)], axis=1) for a in range(4)
    ]
    return jnp.concatenate(rows, axis=0)


def source_picker(owners_ref, slots_ref, pick_ref):
    sub = iota((8, 128), 0)
    lane = iota((8, 128), 1)
    for odd in range(2):
        for half in range(2):
            key = jnp.zeros((8, 128), jnp.int32)
            for t in range(N_TM):
                place = tm_place(t)
                if place // 8 != half:
                    continue
                s = 2 * t + odd
                owner = owners_ref[s // 8]
                device = (owner % 4) * 8 + owner // 4
                channel = device * RECV_DEV + slots_ref[s // 8, s % 8]
                key = jnp.where(sub == place % 8, channel, key)
            found = jnp.concatenate(
                [jnp.where(key == lane, 1.0, 0.0), jnp.where(key == lane + 128, 1.0, 0.0)], axis=1
            )
            for dof in range(2):
                row = (2 * odd + dof) * N_TM + 8 * half
                pick_ref[row : row + 8, :] = found


def whiten_kernel(
    x_hbm, owners_hbm, slots_hbm, y_ref, pick_ref, x_ref, owners_ref, slots_ref, white, pick, sems
):
    is_first = lax.axis_index(ORDER) == 0
    copies = [pltpu.make_async_copy(x_hbm.at[c], x_ref.at[c], sems.at[c]) for c in range(2)]
    small = [
        pltpu.make_async_copy(owners_hbm, owners_ref, sems.at[2]),
        pltpu.make_async_copy(slots_hbm, slots_ref, sems.at[3]),
    ]
    for copy in copies + small:
        copy.start()

    near = band()
    bins = iota((8, F), 1)
    counts = (jnp.minimum(bins + HALF, F - 1) - jnp.maximum(bins - HALF, 0) + 1).astype(f32)
    share = (1.0 / counts)[:1]
    row = iota((256, 256), 0)
    column = iota((256, 256), 1)
    forward = ones_where(row == column)
    backward = ones_where((row + column) % 256 == 0)
    low = iota((256, 128), 1) < 64

    copies[0].wait()
    re = x_ref[0].astype(f32).reshape(WIN * RECV_DEV, F)
    energy = re * re
    copies[1].wait()
    im = x_ref[1].astype(f32).reshape(WIN * RECV_DEV, F)
    energy = energy + im * im
    first = energy.astype(bf16)
    second = (energy - first.astype(f32)).astype(bf16)
    total = dot(first, near) + dot(second, near)
    scale = lax.rsqrt(total * share + EPSILON)
    for c, value in enumerate((re, im)):
        scaled = value * scale
        here = slice(c * WIN * RECV_DEV, (c + 1) * WIN * RECV_DEV)
        for b in range(4):
            white.at[b][here, :] = scaled[:, 128 * b : 128 * (b + 1)]

    for copy in small:
        copy.wait()
    source_picker(owners_ref, slots_ref, pick)
    pick[64:80, :] = jnp.full((16, 256), jnp.where(is_first, 1.0, 0.0), f32)
    pick_ref[...] = pick[...].astype(bf16)

    def by_channel(b):
        strips = [white.at[b][pl.ds(r, 2 * WIN, stride=RECV_DEV), :] for r in range(RECV_DEV)]
        return jnp.concatenate(strips, axis=0).astype(bf16)

    blocks = [by_channel(b) for b in range(4)]
    ahead = dot_nt(forward, jnp.concatenate(blocks[:2], axis=1))
    behind = dot_nt(backward, jnp.concatenate(blocks[2:], axis=1))
    for g in range(4):
        one = ahead[:, 128 * g : 128 * (g + 1)]
        two = behind[:, 128 * g : 128 * (g + 1)]
        even = jnp.where(low, one, pltpu.roll(two, 64, 1)).reshape(N_RECV, 8, 128)
        odd = jnp.where(low, pltpu.roll(one, 64, 1), two).reshape(N_RECV, 8, 128)
        y_ref[:, 16 * g : 16 * (g + 1), :] = jnp.concatenate([even, odd], axis=1).astype(bf16)


def cross_kernel(pick_ref, y_ref, z_ref, wide, tall):
    rows = N_RECV * PAIRS * RECV_DEV
    tall[:rows, :] = y_ref[...].astype(f32).reshape(rows, 128)
    pick = jnp.concatenate([pick_ref[:16, :], pick_ref[32:48, :]], axis=0)
    is_first = pick_ref[64:80, :128].astype(f32)[:1] > 0.5
    lane = iota((N_TM, 128), 1)
    real_lane = (lane // 32) % 2 == 0
    ahead = lane < 64
    sign = jnp.where(real_lane == ahead, -1.0, 1.0)
    nothing = jnp.zeros((64, 128), f32)
    sides = [
        jnp.concatenate(
            [tall[pl.ds(2 * pair + i, 256, stride=8), :] for i in range(2)], axis=1
        ).astype(bf16)
        for pair in range(PAIRS // 2)
    ]
    every = dot(pick, jnp.concatenate(sides, axis=1))
    for pair, side in enumerate(sides):
        found = every[:, 256 * pair : 256 * (pair + 1)]
        lefts = []
        for i in range(2):
            strips = []
            for q in range(4):
                strip = found[N_TM * (q // 2) : N_TM * (q // 2 + 1), 128 * i : 128 * (i + 1)]
                first_bin = jnp.where(ahead == (q % 2 == 0), strip, 0.0)
                if q % 2:
                    strip = sign * jnp.where(
                        real_lane, pltpu.roll(strip, 96, 1), pltpu.roll(strip, 32, 1)
                    )
                if pair == 0 and i == 0:
                    strip = jnp.where(is_first, first_bin, strip)
                strips.append(strip)
            lefts.append(jnp.concatenate(strips, axis=0))
        left = jnp.concatenate(
            [
                jnp.concatenate([lefts[0], nothing], axis=1),
                jnp.concatenate([nothing, lefts[1]], axis=1),
            ],
            axis=0,
        )
        out = dot_nt(left.astype(bf16), side)
        for i in range(2):
            for q in range(4):
                row = 64 * i + N_TM * q
                for h in range(2):
                    wide.at[h][pl.ds(8 * q + 2 * pair + i, N_TM, stride=PITCH), :] = out[
                        row : row + N_TM, 128 * h : 128 * (h + 1)
                    ]
    for h in range(2):
        block = wide[h, : N_TM * PITCH, :].reshape(N_TM, PITCH, 128)[:, :32, :]
        z_ref[:, :, 128 * h : 128 * (h + 1)] = block.astype(bf16).reshape(8, 64, 128)


def gather_kernel(z_ref, q_ref, tall):
    total = jnp.sum(z_ref[...].astype(f32), axis=0)
    for h in range(2):
        tall[128 * h : 128 * (h + 1), :64] = total[:, 128 * h : 128 * (h + 1)].T
    group = iota((N_RECV, 128), 1) // 32
    for h in range(2):
        channels = [tall[pl.ds(4 * h + r, N_RECV, stride=8), :] for r in range(4)]
        for y in range(2):
            packed = jnp.zeros((N_RECV, 128), f32)
            for r in range(4):
                moved = channels[r]
                if r != y:
                    moved = pltpu.roll(moved, (32 * (r - y)) % 128, 1)
                packed = jnp.where(group == r, moved, packed)
            for o in range(4):
                row = 16 * o + 8 * y
                q_ref[row : row + 8, h, :] = packed[8 * o : 8 * (o + 1)]


def lags_kernel(q_ref, wave_ref, out_ref, turned, mixed):
    both = [q_ref[:, h, :].reshape(4, 2, 8, 128) for h in range(2)]
    sums = [(b[:, 0] + b[:, 1]).reshape(N_RECV, 128) for b in both]
    turned[:128, :64] = jnp.concatenate(sums, axis=0).T
    group = iota((8, 128), 1) // 32
    rows = [[], []]
    for q in range(4):
        tiles = [jnp.zeros((8, 128), f32) for _ in range(2)]
        for i in range(4):
            block = turned[pl.ds(4 * q + i, 8, stride=16), :]
            for h in range(2):
                moved = pltpu.roll(block, (32 * (i - h)) % 128, 1) if i != h else block
                tiles[h] = jnp.where(group == i, moved, tiles[h])
        for h in range(2):
            rows[h].append(tiles[h])
    value = jnp.concatenate([jnp.concatenate(r, axis=1) for r in rows], axis=0)
    first = value.astype(bf16)
    second = (value - first.astype(f32)).astype(bf16)
    high = wave_ref[: F // 8].reshape(F, F)
    low = wave_ref[F // 8 :].reshape(F, F)
    both = dot(jnp.concatenate([first, second], axis=0), high)
    lags = both[:16] + (both[16:] + dot(first, low))
    for b in range(4):
        mixed.at[b][:16, :] = lags[:, 128 * b : 128 * (b + 1)]
    for s in range(2):
        for b in range(4):
            out_ref[s, :, 128 * b : 128 * (b + 1)] = mixed.at[b][pl.ds(s, 8, stride=2), :]


VMEM = pl.BlockSpec(memory_space=pltpu.VMEM)
HBM = pl.BlockSpec(memory_space=pltpu.HBM)


def call(kernel, outs, operands, specs, scratch=()):
    return pl.pallas_call(
        kernel,
        out_shape=outs,
        in_specs=specs,
        out_specs=jax.tree.map(lambda _: VMEM, outs),
        scratch_shapes=list(scratch),
        compiler_params=pltpu.CompilerParams(vmem_limit_bytes=32 << 20),
        interpret=INTERPRET,
    )(*operands)


def whiten(spectra, owners, source_slots):
    return call(
        whiten_kernel,
        (
            jax.ShapeDtypeStruct((N_RECV, PAIRS * RECV_DEV, 128), bf16),
            jax.ShapeDtypeStruct((80, 256), bf16),
        ),
        [pltpu.with_memory_space_constraint(a, pltpu.HBM) for a in (spectra, owners, source_slots)],
        [HBM] * 3,
        [
            pltpu.VMEM((2, WIN, RECV_DEV, F), bf16),
            pltpu.SMEM((4,), jnp.int32),
            pltpu.SMEM((4, 8), jnp.int32),
            pltpu.VMEM((4, 2 * WIN * RECV_DEV + 8, 128), f32),
            pltpu.VMEM((80, 256), f32),
            pltpu.SemaphoreType.DMA((4,)),
        ],
    )


def cross(pick, channels):
    return call(
        cross_kernel,
        jax.ShapeDtypeStruct((8, 64, 256), bf16),
        [pick, channels],
        [VMEM, VMEM],
        [
            pltpu.VMEM((2, (N_TM + 1) * PITCH, 128), f32),
            pltpu.VMEM((N_RECV * PAIRS * RECV_DEV + 8, 128), f32),
        ],
    )


def gather(partial):
    return call(
        gather_kernel,
        jax.ShapeDtypeStruct((2 * N_RECV, 2, 128), f32),
        [partial],
        [VMEM],
        [pltpu.VMEM((256 + 8, 128), f32)],
    )


def lags(dofs):
    return call(
        lags_kernel,
        jax.ShapeDtypeStruct((2, RECV_DEV, F), f32),
        [dofs, transform_table()],
        [VMEM] * 2,
        [pltpu.VMEM((128 + 16, 128), f32), pltpu.VMEM((4, 16 + 8, 128), f32)],
    )


def per_device(spectra, owners, source_slots):
    exchange = functools.partial(lax.all_to_all, split_axis=0, concat_axis=0, tiled=True)
    mine, pick = whiten(spectra, owners, source_slots)
    channels = exchange(mine, ORDER)
    partial = exchange(cross(pick, channels), ('core', 'x'))
    return lags(exchange(gather(partial), ("y_lo", "y_hi", "z")))


def solution(mesh):
    names = (*RECV, *TM)
    fine = Mesh(mesh.devices.reshape([SIZES[n] for n in names]), names)
    in_specs = (P(None, TM, RECV, None), P(), P())
    out_specs = P(TM, RECV, None)
    return jax.shard_map(
        per_device, mesh=fine, in_specs=in_specs, out_specs=out_specs, check_vma=False
    )
```
